32 devices in a mesh: island: 2 (over y), fsdp: 16 (over z, x, core).
Axes of the slice: x: 2, y: 2, z: 4, core: 2. Of those that a mesh axis runs over, the one named last changes fastest.
Arguments:
- tokens: bfloat16 [4096, 8192], P(('island', 'fsdp')), may hold values from -6 to 6
- norm_gain: float32 [8192], replicated, may hold values from 0.1 to 1.9
- master: float32 [8192, 512], P('fsdp'), may hold values from -6 to 6
- momentum: float32 [8192, 512], P('fsdp'), may hold values from -4 to 4
- pseudo_grad: float32 [2, 8192, 512], P('island', 'fsdp'), may hold values from -20 to 20
Outputs:
- keys: bfloat16 [4096, 512], P(('island', 'fsdp'))
- master_new: float32 [8192, 512], P('fsdp')
- momentum_new: float32 [8192, 512], P('fsdp')
The draws below stay inside these ranges and needn't reach their ends.
All inputs are finite; a program needn't handle non-finite values.
Results may differ from the reference program's by a relative error of at most 0.008.
Values may be sent and summed in bfloat16 or wider, within the bound.
No kernel may reach another device: no remote copies, remote signals or barrier semaphores. Data moves between devices by JAX's collectives and lax.ppermute only.
A program may use at most 64 MiB of HBM per device.

```python
import math
import jax
import jax.numpy as jnp
from jax import lax

D = 8192
BLOCK = 128
KC = 512
TOKENS = 4096
N_ISLAND = 2


def draw_pseudo_grad(key, part):
    key_base, key_rows, key_cols = jax.random.split(key, 3)
    base = jax.random.normal(key_base, (N_ISLAND, D, KC), jnp.float32)
    row_scale = jnp.exp(jax.random.uniform(key_rows, (1, D, 1), jnp.float32, 0.0, math.log(10.0)))
    col_scale = jnp.exp(jax.random.uniform(key_cols, (1, 1, KC), jnp.float32, 0.0, math.log(10.0)))
    island_scale = 1.0 + 2.0 * jnp.arange(N_ISLAND, dtype=jnp.float32) / (N_ISLAND - 1)
    values = 0.01 * jnp.clip(base, -6.0, 6.0) * row_scale * col_scale * island_scale[:, None, None]
    return values


def block_levels(key, dims, pieces, least, largest):
    factor_of = 1.0
    for position, parts in pieces:
        heights = jax.random.uniform(jax.random.fold_in(jax.random.fold_in(key, 6), position), (parts,), jnp.float32, least / len(pieces), largest / len(pieces))
        factor_of = factor_of * jnp.repeat(jnp.exp(heights), dims[position] // parts).reshape((-1,) + (1,) * (len(dims) - 1 - position))
    return factor_of


def normal_values(key, shape, width, reach, pieces=(), kind=jnp.bfloat16):
    gain = block_levels(key, shape, pieces, -0.22, 0.18) if pieces else 1.0
    entries = jax.random.normal(key, shape, jnp.float32) * width * gain
    return jnp.minimum(jnp.maximum(entries, -reach), reach).astype(kind)


def setup_inputs(seed: int = 0) -> dict:
    splits = jax.random.split(jax.random.key(seed), 6)
    return {
        "tokens": normal_values(splits[0], (TOKENS, D), 1.0, 6.0, ((0, 32),)),
        "norm_gain": jnp.clip(1.0 + 0.18 * jax.random.normal(splits[1], (D,), jnp.float32), 0.1, 1.9),
        "master": normal_values(splits[2], (D, KC), 1.0, 6.0, ((0, 16),), jnp.float32),
        "momentum": normal_values(splits[3], (D, KC), 0.3, 4.0, ((0, 16),), jnp.float32),
        "pseudo_grad": draw_pseudo_grad(jax.random.fold_in(splits[5], 71), 0),
    }


outer_rate = 0.7
outer_mu = 0.9

def reference(tokens, norm_gain, master, momentum, pseudo_grad):
    grouped = pseudo_grad.reshape(N_ISLAND, D, KC // BLOCK, BLOCK)
    peaks = lax.optimization_barrier(jnp.max(jnp.abs(grouped), axis=3))
    shared = lax.optimization_barrier(jnp.sum(peaks, axis=0)) / N_ISLAND + 1e-06
    quantized = jnp.clip(grouped / shared[None, :, :, None], -1.0, 1.0).astype(jnp.bfloat16)
    summed = lax.optimization_barrier(jnp.sum(quantized.astype(jnp.float32), axis=0))
    outer_grad = (shared[:, :, None] * summed / N_ISLAND).reshape(D, KC)
    momentum_new = outer_mu * momentum + outer_grad
    master_new = master - outer_rate * (outer_grad + outer_mu * momentum_new)
    weight = master_new.astype(jnp.bfloat16)
    scale = 1.0 / jnp.sqrt(jnp.float32(D))
    row_count = min(4096, TOKENS)

    def block_keys(row_block):
        features = row_block.astype(jnp.float32)
        inverse = lax.rsqrt(lax.optimization_barrier(jnp.mean(features * features, axis=1, keepdims=True)) + 1e-05)
        normed = (features * inverse * norm_gain[None, :]).astype(jnp.bfloat16)
        product = jnp.dot(normed, weight, preferred_element_type=jnp.float32)
        return (product * scale).astype(jnp.bfloat16)
    blocked = tokens.reshape(TOKENS // row_count, row_count, D)
    keys = lax.map(block_keys, blocked).reshape(TOKENS, KC)
    return (keys, master_new, momentum_new)
```

```python
import functools

import jax
import jax.numpy as jnp
from jax import lax
from jax.experimental import pallas as pl
from jax.experimental.pallas import tpu as pltpu
from jax.sharding import PartitionSpec as P

BLOCK = 128
CORES = 2
RING_LIMIT = 16

outer_rate = 0.7
outer_mu = 0.9
VMEM = pl.BlockSpec(memory_space=pltpu.VMEM)
VMEM_LIMIT = 40 * 1024 * 1024


def params():
    return pltpu.CompilerParams(vmem_limit_bytes=VMEM_LIMIT)


def chip_at(place, chips):
    up = 2 * place
    down = 2 * (chips - 1 - place) + 1
    if isinstance(place, int):
        return up if place < chips // 2 else down
    return jnp.where(place < chips // 2, up, down)


def place_of(chip, chips):
    if isinstance(chip, int):
        return chip // 2 if chip % 2 == 0 else chips - 1 - chip // 2
    return jnp.where(chip % 2 == 0, chip // 2, chips - 1 - chip // 2)


def ring_pairs(chips):
    pairs = []
    for chip in range(chips):
        for core in range(CORES):
            step = 1 if core == 0 else -1
            target = chip_at((place_of(chip, chips) + step) % chips, chips)
            pairs.append((chip * CORES + core, target * CORES + core))
    return pairs


def swap_pairs(chips):
    return [(f, f ^ 1) for f in range(CORES * chips)]


def slots(chips):
    order = [(0, 0), (0, 1)]
    for step in range(1, chips // 2):
        order += [(step, 0), (step, 1), (-step, 1), (-step, 0)]
    return order + [(chips // 2, 0), (chips // 2, 1)]


def shard_of(slot, chips):
    back, other = slot
    me = lax.axis_index("fsdp")
    core = me % CORES
    direction = jnp.where(core == 0, -1, 1)
    place = (place_of(me // CORES, chips) + direction * back + chips) % chips
    return chip_at(place, chips) * CORES + (1 - core if other else core)


def cast_kernel(grad, out):
    out[...] = grad[...].astype(out.dtype)


def cast_half(grad, which):
    rows, cols = grad.shape
    half = rows // 2
    steps = 2
    tall = half // steps
    return pl.pallas_call(
        cast_kernel,
        grid=(steps,),
        in_specs=[pl.BlockSpec((tall, cols), lambda g: (which() * steps + g, 0))],
        out_specs=pl.BlockSpec((tall, cols), lambda g: (g, 0)),
        out_shape=jax.ShapeDtypeStruct((half, cols), jnp.bfloat16),
        compiler_params=params(),
        cost_estimate=pl.CostEstimate(flops=half * cols, bytes_accessed=6 * half * cols, transcendentals=0),
    )(grad)


def mine():
    return lax.axis_index("island")


def others():
    return 1 - lax.axis_index("island")


def token_kernel(chips, half, tokens, own, sent, inverse):
    rows, width = tokens.shape
    for k, slot in enumerate(slots(chips)):
        start = shard_of(slot, chips) * 2 * half
        own[k] = tokens[:, pl.ds(pl.multiple_of(start + mine() * half, half), half)]
        sent[k] = tokens[:, pl.ds(pl.multiple_of(start + others() * half, half), half)]
    total = jnp.zeros((rows, BLOCK), jnp.float32)
    for k in range(width // BLOCK):
        part = tokens[:, k * BLOCK : (k + 1) * BLOCK].astype(jnp.float32)
        total += part * part
    mean = jnp.sum(total, axis=1, keepdims=True) / width
    inverse[...] = lax.rsqrt(mean + 1e-05) / jnp.sqrt(jnp.float32(width))


def split_tokens(tokens, chips):
    rows, width = tokens.shape
    half = width // (chips * CORES * 2)
    shape = (chips * CORES, rows, half)
    return pl.pallas_call(
        functools.partial(token_kernel, chips, half),
        in_specs=[VMEM],
        out_specs=[VMEM] * 3,
        out_shape=[
            jax.ShapeDtypeStruct(shape, tokens.dtype),
            jax.ShapeDtypeStruct(shape, tokens.dtype),
            jax.ShapeDtypeStruct((rows, 1), jnp.float32),
        ],
        compiler_params=params(),
        cost_estimate=pl.CostEstimate(flops=2 * rows * width, bytes_accessed=4 * rows * width, transcendentals=0),
    )(tokens)


def sync_kernel(which, kept, first, second, master, momentum, gain, *refs):
    weight, master_new, momentum_new = refs[-3:]
    tall, cols = first.shape
    row = lax.axis_index("fsdp") * (2 * pl.num_programs(0)) + which() * pl.num_programs(0) + pl.program_id(0)
    gains = jnp.transpose(jnp.broadcast_to(gain[pl.ds(row, 1), :], (tall, tall)))
    for k in range(cols // BLOCK):
        at = slice(k * BLOCK, (k + 1) * BLOCK)
        a = first[:, at].astype(jnp.float32)
        b = second[:, at].astype(jnp.float32)
        peak_a = jnp.max(jnp.abs(a), axis=1, keepdims=True)
        peak_b = jnp.max(jnp.abs(b), axis=1, keepdims=True)
        shared = (peak_a + peak_b) / 2 + 1e-06
        over = 1.0 / shared
        low_a = jnp.clip(a * over, -1.0, 1.0).astype(jnp.bfloat16).astype(jnp.float32)
        low_b = jnp.clip(b * over, -1.0, 1.0).astype(jnp.bfloat16).astype(jnp.float32)
        outer_grad = shared * (low_a + low_b) / 2
        moved = outer_mu * momentum[:, at] + outer_grad
        fresh = master[:, at] - outer_rate * (outer_grad + outer_mu * moved)
        momentum_new[:, at] = moved
        master_new[:, at] = fresh
        if weight is not None:
            weight[:, at] = (gains * fresh).astype(weight.dtype)


def sync_half(which, first, second, master, momentum, gain, kept=()):
    rows, cols = master.shape
    half = rows // 2
    tall = BLOCK
    steps = half // tall
    here = pl.BlockSpec((tall, cols), lambda g: (g, 0))
    there = pl.BlockSpec((tall, cols), lambda g: (which() * steps + g, 0))
    full = jax.ShapeDtypeStruct(master.shape, jnp.float32)
    return pl.pallas_call(
        functools.partial(sync_kernel, which, len(kept)),
        grid=(steps,),
        in_specs=[here, here, there, there, VMEM] + [pl.BlockSpec(memory_space=pl.ANY)] * len(kept),
        out_specs=[here, there, there],
        out_shape=[jax.ShapeDtypeStruct((half, cols), jnp.bfloat16), full, full],
        input_output_aliases={5 + k: 1 + k for k in range(len(kept))},
        compiler_params=params(),
        cost_estimate=pl.CostEstimate(flops=30 * half * cols, bytes_accessed=22 * half * cols, transcendentals=0),
    )(first, second, master, momentum, gain, *kept)


def dot_kernel(slot_from, count, own, other, *refs):
    blocks, more = refs[:count], refs[count:]
    rows = own.shape[1]
    total = more[0][...] if slot_from else None
    for k in range(count):
        left = jnp.concatenate([own[slot_from + k], other[slot_from + k]], axis=0)
        term = jnp.dot(left, blocks[k][...], preferred_element_type=jnp.float32)
        total = term if total is None else total + term
    if slot_from:
        more[1][...] = total[:rows]
        more[2][...] = total[rows:].astype(jnp.bfloat16)
    else:
        more[0][...] = total


def dot_blocks(slot_from, own, other, blocks, total=None):
    rows = own.shape[1]
    cols = blocks[0].shape[1]
    count = len(blocks)
    if total is None:
        outs = jax.ShapeDtypeStruct((2 * rows, cols), jnp.float32)
        out_specs = VMEM
        given = (own, other, *blocks)
    else:
        outs = [jax.ShapeDtypeStruct((rows, cols), jnp.float32), jax.ShapeDtypeStruct((rows, cols), jnp.bfloat16)]
        out_specs = [VMEM, VMEM]
        given = (own, other, *blocks, total)
    return pl.pallas_call(
        functools.partial(dot_kernel, slot_from, count),
        in_specs=[VMEM] * len(given),
        out_specs=out_specs,
        out_shape=outs,
        compiler_params=params(),
        cost_estimate=pl.CostEstimate(
            flops=4 * rows * cols * count * own.shape[2], bytes_accessed=2 * count * own.shape[2] * (cols + 2 * rows), transcendentals=0
        ),
    )(*given)


def close_kernel(mine_part, other_part, inverse, keys):
    keys[...] = ((mine_part[...] + other_part[...].astype(jnp.float32)) * inverse[...]).astype(keys.dtype)


def by_permutes(tokens, norm_gain, master, momentum, pseudo_grad):
    chips = lax.axis_size("fsdp") // CORES
    gain = norm_gain.reshape(-1, BLOCK)
    ring = functools.partial(lax.ppermute, axis_name="fsdp", perm=ring_pairs(chips))
    swap = functools.partial(lax.ppermute, axis_name="fsdp", perm=swap_pairs(chips))
    cross = functools.partial(lax.ppermute, axis_name="island", perm=[(0, 1), (1, 0)])

    grad_sent = cast_half(pseudo_grad[0], others)
    grad_here = cross(grad_sent)
    grad_own = cast_half(pseudo_grad[0], mine)
    own, sent, inverse = split_tokens(tokens, chips)

    weight, master_new, momentum_new = sync_half(mine, grad_own, grad_here, master, momentum, gain)
    sent, weight = lax.optimization_barrier((sent, weight))
    other = cross(sent)
    a = weight
    b = swap(weight)
    blocks = [a, b]
    for step in range(1, chips // 2):
        a, b = ring(a), ring(b)
        blocks += [a, b, swap(a), swap(b)]
    a = ring(a)
    blocks += [a, swap(a)]

    other, grad_own = lax.optimization_barrier((other, grad_own))
    grad_there = cross(grad_own)
    _, master_new, momentum_new = sync_half(
        others, grad_sent, grad_there, master, momentum, gain, (master_new, momentum_new)
    )
    early = len(blocks) - 6
    total = dot_blocks(0, own, other, blocks[:early])
    mine_part, sent_part = dot_blocks(early, own, other, blocks[early:], total)
    other_part = cross(sent_part)
    keys = pl.pallas_call(
        close_kernel,
        in_specs=[VMEM] * 3,
        out_specs=VMEM,
        out_shape=jax.ShapeDtypeStruct(mine_part.shape, jnp.bfloat16),
        compiler_params=params(),
    )(mine_part, other_part, inverse)
    return (keys, master_new, momentum_new)


def by_gathers(tokens, norm_gain, master, momentum, pseudo_grad):
    islands = lax.axis_size("island")
    island_grad = pseudo_grad[0]
    row_total, col_total = island_grad.shape
    every_island = lax.all_gather(
        pseudo_grad.astype(jnp.bfloat16), "island", axis=0, tiled=True
    ).astype(pseudo_grad.dtype)
    grouped_all = every_island.reshape(islands, row_total, col_total // BLOCK, BLOCK)
    peaks_all = jnp.max(jnp.abs(grouped_all), axis=3)
    shared = jnp.sum(peaks_all, axis=0) / islands + 1e-06
    quantized_all = jnp.clip(grouped_all / shared[None, :, :, None], -1.0, 1.0).astype(jnp.bfloat16)
    summed = jnp.sum(quantized_all.astype(jnp.float32), axis=0)
    outer_grad = (shared[:, :, None] * summed / islands).reshape(row_total, col_total)
    momentum_new = outer_mu * momentum + outer_grad
    master_new = master - outer_rate * (outer_grad + outer_mu * momentum_new)
    weight = master_new.astype(jnp.bfloat16)
    features = tokens.astype(jnp.float32)
    inverse = lax.rsqrt(jnp.mean(features * features, axis=1, keepdims=True) + 1e-05)
    normed = (features * inverse * norm_gain[None, :]).astype(jnp.bfloat16)
    scale = 1.0 / jnp.sqrt(jnp.float32(normed.shape[1]))
    gathered = lax.all_gather(weight, "fsdp", axis=0, tiled=True)
    product = jnp.dot(normed, gathered, preferred_element_type=jnp.float32)
    keys = (product * scale).astype(jnp.bfloat16)
    return (keys, master_new, momentum_new)


def on_device(tokens, norm_gain, master, momentum, pseudo_grad):
    shards = lax.axis_size("fsdp")
    rows = master.shape[0]
    ringed = shards % (2 * CORES) == 0 and 4 * CORES <= shards <= RING_LIMIT * CORES
    if lax.axis_size("island") == 2 and ringed and rows % (2 * BLOCK) == 0:
        return by_permutes(tokens, norm_gain, master, momentum, pseudo_grad)
    return by_gathers(tokens, norm_gain, master, momentum, pseudo_grad)


def solution(mesh):
    placed = (
        P(("island", "fsdp"), None),
        P(),
        P("fsdp", None),
        P("fsdp", None),
        P("island", "fsdp", None),
    )
    return jax.shard_map(
        on_device,
        mesh=mesh,
        in_specs=placed,
        out_specs=(P(("island", "fsdp"), None), P("fsdp", None), P("fsdp", None)),
        check_vma=False,
    )
```

```python
import functools

import jax
import jax.numpy as jnp
from jax import lax
from jax.experimental import pallas as pl
from jax.experimental.pallas import tpu as pltpu
from jax.sharding import PartitionSpec as P

BLOCK = 128
CORES = 2
RING_LIMIT = 16

outer_rate = 0.7
outer_mu = 0.9
VMEM = pl.BlockSpec(memory_space=pltpu.VMEM)
VMEM_LIMIT = 40 * 1024 * 1024


def params():
    return pltpu.CompilerParams(vmem_limit_bytes=VMEM_LIMIT)


def chip_at(place, chips):
    up = 2 * place
    down = 2 * (chips - 1 - place) + 1
    if isinstance(place, int):
        return up if place < chips // 2 else down
    return jnp.where(place < chips // 2, up, down)


def place_of(chip, chips):
    if isinstance(chip, int):
        return chip // 2 if chip % 2 == 0 else chips - 1 - chip // 2
    return jnp.where(chip % 2 == 0, chip // 2, chips - 1 - chip // 2)


def ring_pairs(chips):
    pairs = []
    for chip in range(chips):
        for core in range(CORES):
            step = 1 if core == 0 else -1
            target = chip_at((place_of(chip, chips) + step) % chips, chips)
            pairs.append((chip * CORES + core, target * CORES + core))
    return pairs


def swap_pairs(chips):
    return [(f, f ^ 1) for f in range(CORES * chips)]


def slots(chips):
    shared = []
    for step in range(1, chips // 2):
        shared += [(step, 0), (step, 1), (-step, 1), (-step, 0)]
    return shared + [(chips // 2, 0), (chips // 2, 1)], [(0, 0), (0, 1)]


def shard_of(slot, chips):
    back, other = slot
    me = lax.axis_index("fsdp")
    core = me % CORES
    direction = jnp.where(core == 0, -1, 1)
    place = (place_of(me // CORES, chips) + direction * back + chips) % chips
    return chip_at(place, chips) * CORES + (1 - core if other else core)


def cast_kernel(grad, out):
    out[...] = grad[...].astype(out.dtype)


def cast_half(grad, which):
    rows, cols = grad.shape
    half = rows // 2
    steps = 2
    tall = half // steps
    return pl.pallas_call(
        cast_kernel,
        grid=(steps,),
        in_specs=[pl.BlockSpec((tall, cols), lambda g: (which() * steps + g, 0))],
        out_specs=pl.BlockSpec((tall, cols), lambda g: (g, 0)),
        out_shape=jax.ShapeDtypeStruct((half, cols), jnp.bfloat16),
        compiler_params=params(),
        cost_estimate=pl.CostEstimate(flops=half * cols, bytes_accessed=6 * half * cols, transcendentals=0),
    )(grad)


def mine():
    return lax.axis_index("island")


def others():
    return 1 - lax.axis_index("island")


def token_kernel(chips, half, tokens, own, sent, whole, inverse):
    rows, width = tokens.shape
    shared, kept = slots(chips)

    def columns(slot, which):
        start = shard_of(slot, chips) * 2 * half + which * half
        return tokens[:, pl.ds(pl.multiple_of(start, half), half)]

    for k, slot in enumerate(shared):
        own[k] = columns(slot, mine())
        sent[k] = columns(slot, others())
    for k, slot in enumerate(kept):
        whole[2 * k] = columns(slot, mine())
        whole[2 * k + 1] = columns(slot, others())
    total = jnp.zeros((rows, BLOCK), jnp.float32)
    for k in range(width // BLOCK):
        part = tokens[:, k * BLOCK : (k + 1) * BLOCK].astype(jnp.float32)
        total += part * part
    mean = jnp.sum(total, axis=1, keepdims=True) / width
    inverse[...] = lax.rsqrt(mean + 1e-05) / jnp.sqrt(jnp.float32(width))


def split_tokens(tokens, chips):
    rows, width = tokens.shape
    half = width // (chips * CORES * 2)
    shared, kept = slots(chips)
    split = jax.ShapeDtypeStruct((len(shared), rows, half), tokens.dtype)
    whole = jax.ShapeDtypeStruct((2 * len(kept), rows, half), tokens.dtype)
    return pl.pallas_call(
        functools.partial(token_kernel, chips, half),
        in_specs=[VMEM],
        out_specs=[VMEM] * 4,
        out_shape=[split, split, whole, jax.ShapeDtypeStruct((rows, 1), jnp.float32)],
        compiler_params=params(),
        cost_estimate=pl.CostEstimate(flops=2 * rows * width, bytes_accessed=4 * rows * width, transcendentals=0),
    )(tokens)


def synced(a, b):
    a, b = a.astype(jnp.float32), b.astype(jnp.float32)
    peak_a = jnp.max(jnp.abs(a), axis=1, keepdims=True)
    peak_b = jnp.max(jnp.abs(b), axis=1, keepdims=True)
    shared = (peak_a + peak_b) / 2 + 1e-06
    over = 1.0 / shared
    low_a = jnp.clip(a * over, -1.0, 1.0).astype(jnp.bfloat16).astype(jnp.float32)
    low_b = jnp.clip(b * over, -1.0, 1.0).astype(jnp.bfloat16).astype(jnp.float32)
    return shared * (low_a + low_b) / 2


def gains_of(gain, row):
    return jnp.transpose(jnp.broadcast_to(gain[pl.ds(row // BLOCK, 1), :], (BLOCK, BLOCK)))


def weight_kernel(which, first, second, master, momentum, gain, weight):
    half, cols = first.shape
    base = lax.axis_index("fsdp") * (2 * half)
    for start in range(0, half, BLOCK):
        rows = slice(start, start + BLOCK)
        there = which() * half + start
        held = pl.ds(pl.multiple_of(there, BLOCK), BLOCK)
        gains = gains_of(gain, base + there)
        for col in range(0, cols, BLOCK):
            at = slice(col, col + BLOCK)
            outer_grad = synced(first[rows, at], second[rows, at])
            moved = outer_mu * momentum[held, at] + outer_grad
            fresh = master[held, at] - outer_rate * (outer_grad + outer_mu * moved)
            weight[rows, at] = (gains * fresh).astype(weight.dtype)


def sync_weight(which, first, second, master, momentum, gain):
    half, cols = first.shape
    return pl.pallas_call(
        functools.partial(weight_kernel, which),
        in_specs=[VMEM] * 5,
        out_specs=VMEM,
        out_shape=jax.ShapeDtypeStruct((half, cols), jnp.bfloat16),
        compiler_params=params(),
        cost_estimate=pl.CostEstimate(
            flops=30 * half * cols, bytes_accessed=14 * half * cols, transcendentals=0
        ),
    )(first, second, master, momentum, gain)


def outer_kernel(here_a, here_b, there_a, there_b, master, momentum, master_new, momentum_new):
    half, cols = here_a.shape
    for which, a, b in ((mine(), here_a, here_b), (others(), there_a, there_b)):
        for start in range(0, half, BLOCK):
            rows = slice(start, start + BLOCK)
            held = pl.ds(pl.multiple_of(which * half + start, BLOCK), BLOCK)
            for col in range(0, cols, BLOCK):
                at = slice(col, col + BLOCK)
                outer_grad = synced(a[rows, at], b[rows, at])
                moved = outer_mu * momentum[held, at] + outer_grad
                momentum_new[held, at] = moved
                master_new[held, at] = master[held, at] - outer_rate * (outer_grad + outer_mu * moved)


def sync_outer(here_a, here_b, there_a, there_b, master, momentum):
    rows, cols = master.shape
    full = jax.ShapeDtypeStruct(master.shape, jnp.float32)
    return pl.pallas_call(
        outer_kernel,
        in_specs=[VMEM] * 6,
        out_specs=[VMEM] * 2,
        out_shape=[full, full],
        compiler_params=params(),
        cost_estimate=pl.CostEstimate(flops=30 * rows * cols, bytes_accessed=20 * rows * cols, transcendentals=0),
    )(here_a, here_b, there_a, there_b, master, momentum)


def cost_of(blocks, rows):
    depth, cols = blocks[0].shape
    count = len(blocks)
    return pl.CostEstimate(
        flops=2 * rows * cols * depth * count, bytes_accessed=2 * count * depth * (cols + rows), transcendentals=0
    )


def own_kernel(first, count, whole, *refs):
    blocks, out = refs[:count], refs[-1]
    total = refs[count][...] if len(refs) > count + 1 else jnp.zeros(out.shape, jnp.float32)
    for k, block in enumerate(blocks):
        total += jnp.dot(whole[first + k], block[...], preferred_element_type=jnp.float32)
    out[...] = total


def dot_own(first, whole, blocks, *total):
    return pl.pallas_call(
        functools.partial(own_kernel, first, len(blocks)),
        in_specs=[VMEM] * (1 + len(blocks) + len(total)),
        out_specs=VMEM,
        out_shape=jax.ShapeDtypeStruct((whole.shape[1], blocks[0].shape[1]), jnp.float32),
        compiler_params=params(),
        cost_estimate=cost_of(blocks, whole.shape[1]),
    )(whole, *blocks, *total)


def early_kernel(own, other, *refs):
    *blocks, total = refs
    total[...] = jnp.zeros(total.shape, jnp.float32)
    for k, block in enumerate(blocks):
        left = jnp.concatenate([own[k], other[k]], axis=0)
        total[...] += jnp.dot(left, block[...], preferred_element_type=jnp.float32)


def dot_early(own, other, blocks):
    shape = (2 * own.shape[1], blocks[0].shape[1])
    return pl.pallas_call(
        early_kernel,
        in_specs=[VMEM] * (2 + len(blocks)),
        out_specs=VMEM,
        out_shape=jax.ShapeDtypeStruct(shape, jnp.float32),
        compiler_params=params(),
        cost_estimate=cost_of(blocks, shape[0]),
    )(own, other, *blocks)


def late_kernel(first, own, other, early, *refs):
    *blocks, mine_part, sent_part = refs
    rows = own.shape[1]
    total = early[...]
    for k, block in enumerate(blocks):
        left = jnp.concatenate([own[first + k], other[first + k]], axis=0)
        total += jnp.dot(left, block[...], preferred_element_type=jnp.float32)
    mine_part[...] = total[:rows]
    sent_part[...] = total[rows:].astype(sent_part.dtype)


def dot_late(first, own, other, early, blocks):
    shape = (own.shape[1], blocks[0].shape[1])
    return pl.pallas_call(
        functools.partial(late_kernel, first),
        in_specs=[VMEM] * (3 + len(blocks)),
        out_specs=[VMEM] * 2,
        out_shape=[jax.ShapeDtypeStruct(shape, jnp.float32), jax.ShapeDtypeStruct(shape, jnp.bfloat16)],
        compiler_params=params(),
        cost_estimate=cost_of(blocks, 2 * shape[0]),
    )(own, other, early, *blocks)


def close_kernel(own_part, mine_part, other_part, inverse, keys):
    total = own_part[...] + mine_part[...] + other_part[...].astype(jnp.float32)
    keys[...] = (total * inverse[...]).astype(keys.dtype)


def close(own_part, mine_part, other_part, inverse):
    return pl.pallas_call(
        close_kernel,
        in_specs=[VMEM] * 4,
        out_specs=VMEM,
        out_shape=jax.ShapeDtypeStruct(mine_part.shape, jnp.bfloat16),
        compiler_params=params(),
    )(own_part, mine_part, other_part, inverse)


def by_permutes(tokens, norm_gain, master, momentum, pseudo_grad):
    chips = lax.axis_size("fsdp") // CORES
    ring = functools.partial(lax.ppermute, axis_name="fsdp", perm=ring_pairs(chips))
    swap = functools.partial(lax.ppermute, axis_name="fsdp", perm=swap_pairs(chips))
    cross = functools.partial(lax.ppermute, axis_name="island", perm=[(0, 1), (1, 0)])
    tie = lax.optimization_barrier

    gain = norm_gain.reshape(-1, BLOCK)
    grad_sent = cast_half(pseudo_grad[0], others)
    grad_here = cross(grad_sent)
    grad_own = cast_half(pseudo_grad[0], mine)
    grad_there = cross(grad_own)
    own, sent, whole, inverse = split_tokens(tokens, chips)
    grad_here, own = tie((grad_here, own))

    a = weight = sync_weight(mine, grad_own, grad_here, master, momentum, gain)
    weight_over = sync_weight(others, grad_sent, grad_there, master, momentum, gain)
    near_over = swap(weight_over)
    b = near = swap(weight)
    other = cross(sent)
    blocks = []
    for step in range(1, chips // 2):
        a, b = ring(a), ring(b)
        if step == 1:
            b, near_over = tie((b, near_over))
        blocks += [a, b, swap(a), swap(b)]
    a = ring(a)
    late = [a, swap(a)]

    master_new, momentum_new = sync_outer(grad_own, grad_here, grad_sent, grad_there, master, momentum)
    early = dot_early(own, other, blocks)
    mine_part, sent_part = dot_late(len(blocks), own, other, early, late)
    other_part = cross(sent_part)
    own_part = dot_own(0, whole, [weight, weight_over, near, near_over])
    keys = close(own_part, mine_part, other_part, inverse)
    return (keys, master_new, momentum_new)


def by_gathers(tokens, norm_gain, master, momentum, pseudo_grad):
    islands = lax.axis_size("island")
    island_grad = pseudo_grad[0]
    row_total, col_total = island_grad.shape
    every_island = lax.all_gather(
        pseudo_grad.astype(jnp.bfloat16), "island", axis=0, tiled=True
    ).astype(pseudo_grad.dtype)
    grouped_all = every_island.reshape(islands, row_total, col_total // BLOCK, BLOCK)
    peaks_all = jnp.max(jnp.abs(grouped_all), axis=3)
    shared = jnp.sum(peaks_all, axis=0) / islands + 1e-06
    quantized_all = jnp.clip(grouped_all / shared[None, :, :, None], -1.0, 1.0).astype(jnp.bfloat16)
    summed = jnp.sum(quantized_all.astype(jnp.float32), axis=0)
    outer_grad = (shared[:, :, None] * summed / islands).reshape(row_total, col_total)
    momentum_new = outer_mu * momentum + outer_grad
    master_new = master - outer_rate * (outer_grad + outer_mu * momentum_new)
    weight = master_new.astype(jnp.bfloat16)
    features = tokens.astype(jnp.float32)
    inverse = lax.rsqrt(jnp.mean(features * features, axis=1, keepdims=True) + 1e-05)
    normed = (features * inverse * norm_gain[None, :]).astype(jnp.bfloat16)
    scale = 1.0 / jnp.sqrt(jnp.float32(normed.shape[1]))
    gathered = lax.all_gather(weight, "fsdp", axis=0, tiled=True)
    product = jnp.dot(normed, gathered, preferred_element_type=jnp.float32)
    keys = (product * scale).astype(jnp.bfloat16)
    return (keys, master_new, momentum_new)


def on_device(tokens, norm_gain, master, momentum, pseudo_grad):
    shards = lax.axis_size("fsdp")
    rows = master.shape[0]
    ringed = shards % (2 * CORES) == 0 and 4 * CORES <= shards <= RING_LIMIT * CORES
    if lax.axis_size("island") == 2 and ringed and rows % (2 * BLOCK) == 0:
        return by_permutes(tokens, norm_gain, master, momentum, pseudo_grad)
    return by_gathers(tokens, norm_gain, master, momentum, pseudo_grad)


def solution(mesh):
    placed = (
        P(("island", "fsdp"), None),
        P(),
        P("fsdp", None),
        P("fsdp", None),
        P("island", "fsdp", None),
    )
    return jax.shard_map(
        on_device,
        mesh=mesh,
        in_specs=placed,
        out_specs=(P(("island", "fsdp"), None), P("fsdp", None), P("fsdp", None)),
        check_vma=False,
    )
```

```python
import functools

import jax
import jax.numpy as jnp
from jax import lax
from jax.experimental import pallas as pl
from jax.experimental.pallas import tpu as pltpu
from jax.sharding import PartitionSpec as P

BLOCK = 128
CORES = 2
RING_LIMIT = 16
EARLY = 10

outer_rate = 0.7
outer_mu = 0.9
VMEM = pl.BlockSpec(memory_space=pltpu.VMEM)
VMEM_LIMIT = 40 * 1024 * 1024


def params():
    return pltpu.CompilerParams(vmem_limit_bytes=VMEM_LIMIT)


def chip_at(place, chips):
    up = 2 * place
    down = 2 * (chips - 1 - place) + 1
    if isinstance(place, int):
        return up if place < chips // 2 else down
    return jnp.where(place < chips // 2, up, down)


def place_of(chip, chips):
    if isinstance(chip, int):
        return chip // 2 if chip % 2 == 0 else chips - 1 - chip // 2
    return jnp.where(chip % 2 == 0, chip // 2, chips - 1 - chip // 2)


def ring_pairs(chips):
    pairs = []
    for chip in range(chips):
        for core in range(CORES):
            step = 1 if core == 0 else -1
            target = chip_at((place_of(chip, chips) + step) % chips, chips)
            pairs.append((chip * CORES + core, target * CORES + core))
    return pairs


def swap_pairs(chips):
    return [(f, f ^ 1) for f in range(CORES * chips)]


def slots(chips):
    shared = []
    for step in range(1, chips // 2):
        shared += [(step, 0), (step, 1), (-step, 1), (-step, 0)]
    return shared + [(chips // 2, 0), (chips // 2, 1)], [(0, 0), (0, 1)]


def shard_of(slot, chips):
    back, other = slot
    me = lax.axis_index("fsdp")
    core = me % CORES
    direction = jnp.where(core == 0, -1, 1)
    place = (place_of(me // CORES, chips) + direction * back + chips) % chips
    return chip_at(place, chips) * CORES + (1 - core if other else core)


def cast_kernel(grad, out):
    out[...] = grad[...].astype(out.dtype)


def cast_half(grad, which):
    rows, cols = grad.shape
    half = rows // 2
    steps = 2
    tall = half // steps
    return pl.pallas_call(
        cast_kernel,
        grid=(steps,),
        in_specs=[pl.BlockSpec((tall, cols), lambda g: (which() * steps + g, 0))],
        out_specs=pl.BlockSpec((tall, cols), lambda g: (g, 0)),
        out_shape=jax.ShapeDtypeStruct((half, cols), jnp.bfloat16),
        compiler_params=params(),
        cost_estimate=pl.CostEstimate(flops=half * cols, bytes_accessed=6 * half * cols, transcendentals=0),
    )(grad)


def mine():
    return lax.axis_index("island")


def others():
    return 1 - lax.axis_index("island")


def tiles(shape, tall, wide):
    rows, cols = shape
    return [(slice(r, r + tall), slice(c, c + wide)) for r in range(0, rows, tall) for c in range(0, cols, wide)]


def token_kernel(chips, half, early, tokens, grad, own, sent_early, sent_late, whole, inverse):
    rows, width = tokens.shape
    shared, kept = slots(chips)

    def columns(slot, which):
        start = shard_of(slot, chips) * 2 * half + which * half
        return tokens[:, pl.ds(pl.multiple_of(start, half), half)]

    for k, slot in enumerate(shared):
        own[k] = columns(slot, mine())
        if k < early:
            sent_early[k] = columns(slot, others())
        else:
            sent_late[k - early] = columns(slot, others())
    for k, at in enumerate(tiles(grad.shape, rows, half)):
        sent_early[early + k] = grad[at]
    for k, slot in enumerate(kept):
        whole[2 * k] = columns(slot, mine())
        whole[2 * k + 1] = columns(slot, others())
    total = jnp.zeros((rows, BLOCK), jnp.float32)
    for k in range(width // BLOCK):
        part = tokens[:, k * BLOCK : (k + 1) * BLOCK].astype(jnp.float32)
        total += part * part
    mean = jnp.sum(total, axis=1, keepdims=True) / width
    inverse[...] = lax.rsqrt(mean + 1e-05) / jnp.sqrt(jnp.float32(width))


def split_tokens(tokens, grad, chips, early):
    rows, width = tokens.shape
    half = width // (chips * CORES * 2)
    shared, kept = slots(chips)
    counts = len(shared), early + len(tiles(grad.shape, rows, half)), len(shared) - early, 2 * len(kept)
    return pl.pallas_call(
        functools.partial(token_kernel, chips, half, early),
        in_specs=[VMEM] * 2,
        out_specs=[VMEM] * 5,
        out_shape=[jax.ShapeDtypeStruct((count, rows, half), tokens.dtype) for count in counts]
        + [jax.ShapeDtypeStruct((rows, 1), jnp.float32)],
        compiler_params=params(),
        cost_estimate=pl.CostEstimate(flops=2 * rows * width, bytes_accessed=4 * rows * width, transcendentals=0),
    )(tokens, grad)


def unpack_kernel(first, packed, grad):
    for k, at in enumerate(tiles(grad.shape, *packed.shape[1:])):
        grad[at] = packed[first + k]


def unpack(first, packed, shape):
    return pl.pallas_call(
        functools.partial(unpack_kernel, first),
        in_specs=[VMEM],
        out_specs=VMEM,
        out_shape=jax.ShapeDtypeStruct(shape, packed.dtype),
        compiler_params=params(),
        cost_estimate=pl.CostEstimate(flops=0, bytes_accessed=4 * shape[0] * shape[1], transcendentals=0),
    )(packed)


def synced(a, b):
    a, b = a.astype(jnp.float32), b.astype(jnp.float32)
    peak_a = jnp.max(jnp.abs(a), axis=1, keepdims=True)
    peak_b = jnp.max(jnp.abs(b), axis=1, keepdims=True)
    shared = (peak_a + peak_b) / 2 + 1e-06
    over = 1.0 / shared
    low_a = jnp.clip(a * over, -1.0, 1.0).astype(jnp.bfloat16).astype(jnp.float32)
    low_b = jnp.clip(b * over, -1.0, 1.0).astype(jnp.bfloat16).astype(jnp.float32)
    return shared * (low_a + low_b) / 2


def gains_of(gain, row):
    return jnp.transpose(jnp.broadcast_to(gain[pl.ds(row // BLOCK, 1), :], (BLOCK, BLOCK)))


def weight_kernel(which, first, second, master, momentum, gain, weight):
    half, cols = first.shape
    base = lax.axis_index("fsdp") * (2 * half)
    for start in range(0, half, BLOCK):
        rows = slice(start, start + BLOCK)
        there = which() * half + start
        held = pl.ds(pl.multiple_of(there, BLOCK), BLOCK)
        gains = gains_of(gain, base + there)
        for col in range(0, cols, BLOCK):
            at = slice(col, col + BLOCK)
            outer_grad = synced(first[rows, at], second[rows, at])
            moved = outer_mu * momentum[held, at] + outer_grad
            fresh = master[held, at] - outer_rate * (outer_grad + outer_mu * moved)
            weight[rows, at] = (gains * fresh).astype(weight.dtype)


def sync_weight(which, first, second, master, momentum, gain):
    half, cols = first.shape
    return pl.pallas_call(
        functools.partial(weight_kernel, which),
        in_specs=[VMEM] * 5,
        out_specs=VMEM,
        out_shape=jax.ShapeDtypeStruct((half, cols), jnp.bfloat16),
        compiler_params=params(),
        cost_estimate=pl.CostEstimate(
            flops=30 * half * cols, bytes_accessed=14 * half * cols, transcendentals=0
        ),
    )(first, second, master, momentum, gain)


def outer_kernel(here_a, here_b, there_a, there_b, master, momentum, master_new, momentum_new):
    half, cols = here_a.shape
    for which, a, b in ((mine(), here_a, here_b), (others(), there_a, there_b)):
        for start in range(0, half, BLOCK):
            rows = slice(start, start + BLOCK)
            held = pl.ds(pl.multiple_of(which * half + start, BLOCK), BLOCK)
            for col in range(0, cols, BLOCK):
                at = slice(col, col + BLOCK)
                outer_grad = synced(a[rows, at], b[rows, at])
                moved = outer_mu * momentum[held, at] + outer_grad
                momentum_new[held, at] = moved
                master_new[held, at] = master[held, at] - outer_rate * (outer_grad + outer_mu * moved)


def sync_outer(here_a, here_b, there_a, there_b, master, momentum):
    rows, cols = master.shape
    full = jax.ShapeDtypeStruct(master.shape, jnp.float32)
    return pl.pallas_call(
        outer_kernel,
        in_specs=[VMEM] * 6,
        out_specs=[VMEM] * 2,
        out_shape=[full, full],
        compiler_params=params(),
        cost_estimate=pl.CostEstimate(flops=30 * rows * cols, bytes_accessed=20 * rows * cols, transcendentals=0),
    )(here_a, here_b, there_a, there_b, master, momentum)


def cost_of(blocks, rows):
    depth, cols = blocks[0].shape
    count = len(blocks)
    return pl.CostEstimate(
        flops=2 * rows * cols * depth * count, bytes_accessed=2 * count * depth * (cols + rows), transcendentals=0
    )


def own_kernel(first, count, whole, *refs):
    blocks, out = refs[:count], refs[-1]
    total = refs[count][...] if len(refs) > count + 1 else jnp.zeros(out.shape, jnp.float32)
    for k, block in enumerate(blocks):
        total += jnp.dot(whole[first + k], block[...], preferred_element_type=jnp.float32)
    out[...] = total


def dot_own(first, whole, blocks, *total):
    return pl.pallas_call(
        functools.partial(own_kernel, first, len(blocks)),
        in_specs=[VMEM] * (1 + len(blocks) + len(total)),
        out_specs=VMEM,
        out_shape=jax.ShapeDtypeStruct((whole.shape[1], blocks[0].shape[1]), jnp.float32),
        compiler_params=params(),
        cost_estimate=cost_of(blocks, whole.shape[1]),
    )(whole, *blocks, *total)


def pair_of(own, others, k):
    first, second = others
    count = own.shape[0] - second.shape[0]
    return jnp.concatenate([own[k], first[k] if k < count else second[k - count]], axis=0)


def early_kernel(start, count, own, first, second, *refs):
    blocks, total = refs[:count], refs[-1]
    total[...] = refs[count][...] if len(refs) > count + 1 else jnp.zeros(total.shape, jnp.float32)
    for k, block in enumerate(blocks):
        total[...] += jnp.dot(pair_of(own, (first, second), start + k), block[...], preferred_element_type=jnp.float32)


def dot_early(start, own, others, blocks, *total):
    shape = (2 * own.shape[1], blocks[0].shape[1])
    return pl.pallas_call(
        functools.partial(early_kernel, start, len(blocks)),
        in_specs=[VMEM] * (3 + len(blocks) + len(total)),
        out_specs=VMEM,
        out_shape=jax.ShapeDtypeStruct(shape, jnp.float32),
        compiler_params=params(),
        cost_estimate=cost_of(blocks, shape[0]),
    )(own, *others, *blocks, *total)


def late_kernel(start, own, first, second, early, *refs):
    *blocks, mine_part, sent_part = refs
    rows = own.shape[1]
    total = early[...]
    for k, block in enumerate(blocks):
        total += jnp.dot(pair_of(own, (first, second), start + k), block[...], preferred_element_type=jnp.float32)
    mine_part[...] = total[:rows]
    sent_part[...] = total[rows:].astype(sent_part.dtype)


def dot_late(start, own, others, early, blocks):
    shape = (own.shape[1], blocks[0].shape[1])
    return pl.pallas_call(
        functools.partial(late_kernel, start),
        in_specs=[VMEM] * (4 + len(blocks)),
        out_specs=[VMEM] * 2,
        out_shape=[jax.ShapeDtypeStruct(shape, jnp.float32), jax.ShapeDtypeStruct(shape, jnp.bfloat16)],
        compiler_params=params(),
        cost_estimate=cost_of(blocks, 2 * shape[0]),
    )(own, *others, early, *blocks)


def close_kernel(own_part, mine_part, other_part, inverse, keys):
    total = own_part[...] + mine_part[...] + other_part[...].astype(jnp.float32)
    keys[...] = (total * inverse[...]).astype(keys.dtype)


def close(own_part, mine_part, other_part, inverse):
    return pl.pallas_call(
        close_kernel,
        in_specs=[VMEM] * 4,
        out_specs=VMEM,
        out_shape=jax.ShapeDtypeStruct(mine_part.shape, jnp.bfloat16),
        compiler_params=params(),
    )(own_part, mine_part, other_part, inverse)


def by_permutes(tokens, norm_gain, master, momentum, pseudo_grad):
    chips = lax.axis_size("fsdp") // CORES
    ring = functools.partial(lax.ppermute, axis_name="fsdp", perm=ring_pairs(chips))
    swap = functools.partial(lax.ppermute, axis_name="fsdp", perm=swap_pairs(chips))
    cross = functools.partial(lax.ppermute, axis_name="island", perm=[(0, 1), (1, 0)])
    tie = lax.optimization_barrier

    gain = norm_gain.reshape(-1, BLOCK)
    grad_sent = cast_half(pseudo_grad[0], others)
    grad_here = cross(grad_sent)
    grad_own = cast_half(pseudo_grad[0], mine)
    early = EARLY
    own, sent_early, sent_late, whole, inverse = split_tokens(tokens, grad_own, chips, early)
    grad_here, own = tie((grad_here, own))
    other_early, other_late = cross(sent_early), cross(sent_late)

    a = weight = sync_weight(mine, grad_own, grad_here, master, momentum, gain)
    b = near = swap(weight)
    chains = []
    for step in range(1, chips // 2):
        a, b = ring(a), ring(b)
        chains.append((a, b))
    a, other_early = tie((a, other_early))
    chains[-1] = (a, b)
    grad_there = unpack(early, other_early, grad_own.shape)
    weight_over = sync_weight(others, grad_sent, grad_there, master, momentum, gain)
    last, weight_over = tie((b, weight_over))
    blocks = []
    for k, (a, b) in enumerate(chains):
        blocks += [a, b, swap(a), swap(last if k == len(chains) - 1 else b)]
    a = ring(a)
    late = [a, swap(a)]

    own_part = dot_own(0, whole, [weight, weight_over, near, swap(weight_over)])
    master_new, momentum_new = sync_outer(grad_own, grad_here, grad_sent, grad_there, master, momentum)
    crossed = (other_early, other_late)
    total = dot_early(0, own, crossed, blocks)
    mine_part, sent_part = dot_late(len(blocks), own, crossed, total, late)
    keys = close(own_part, mine_part, cross(sent_part), inverse)
    return (keys, master_new, momentum_new)


def by_gathers(tokens, norm_gain, master, momentum, pseudo_grad):
    islands = lax.axis_size("island")
    island_grad = pseudo_grad[0]
    row_total, col_total = island_grad.shape
    every_island = lax.all_gather(
        pseudo_grad.astype(jnp.bfloat16), "island", axis=0, tiled=True
    ).astype(pseudo_grad.dtype)
    grouped_all = every_island.reshape(islands, row_total, col_total // BLOCK, BLOCK)
    peaks_all = jnp.max(jnp.abs(grouped_all), axis=3)
    shared = jnp.sum(peaks_all, axis=0) / islands + 1e-06
    quantized_all = jnp.clip(grouped_all / shared[None, :, :, None], -1.0, 1.0).astype(jnp.bfloat16)
    summed = jnp.sum(quantized_all.astype(jnp.float32), axis=0)
    outer_grad = (shared[:, :, None] * summed / islands).reshape(row_total, col_total)
    momentum_new = outer_mu * momentum + outer_grad
    master_new = master - outer_rate * (outer_grad + outer_mu * momentum_new)
    weight = master_new.astype(jnp.bfloat16)
    features = tokens.astype(jnp.float32)
    inverse = lax.rsqrt(jnp.mean(features * features, axis=1, keepdims=True) + 1e-05)
    normed = (features * inverse * norm_gain[None, :]).astype(jnp.bfloat16)
    scale = 1.0 / jnp.sqrt(jnp.float32(normed.shape[1]))
    gathered = lax.all_gather(weight, "fsdp", axis=0, tiled=True)
    product = jnp.dot(normed, gathered, preferred_element_type=jnp.float32)
    keys = (product * scale).astype(jnp.bfloat16)
    return (keys, master_new, momentum_new)


def on_device(tokens, norm_gain, master, momentum, pseudo_grad):
    shards = lax.axis_size("fsdp")
    rows = master.shape[0]
    ringed = shards % (2 * CORES) == 0 and 4 * CORES <= shards <= RING_LIMIT * CORES
    tiled = tokens.shape[0] == BLOCK and rows % (2 * BLOCK) == 0 and 2 * master.shape[1] % rows == 0
    if lax.axis_size("island") == 2 and ringed and tiled:
        return by_permutes(tokens, norm_gain, master, momentum, pseudo_grad)
    return by_gathers(tokens, norm_gain, master, momentum, pseudo_grad)


def solution(mesh):
    placed = (
        P(("island", "fsdp"), None),
        P(),
        P("fsdp", None),
        P("fsdp", None),
        P("island", "fsdp", None),
    )
    return jax.shard_map(
        on_device,
        mesh=mesh,
        in_specs=placed,
        out_specs=(P(("island", "fsdp"), None), P("fsdp", None), P("fsdp", None)),
        check_vma=False,
    )
```

```python
import functools

import jax
import jax.numpy as jnp
from jax import lax
from jax.experimental import pallas as pl
from jax.experimental.pallas import tpu as pltpu
from jax.sharding import PartitionSpec as P

BLOCK = 128
CORES = 2
RING_LIMIT = 16

outer_rate = 0.7
outer_mu = 0.9
VMEM = pl.BlockSpec(memory_space=pltpu.VMEM)
VMEM_LIMIT = 40 * 1024 * 1024


def params():
    return pltpu.CompilerParams(vmem_limit_bytes=VMEM_LIMIT)


def chip_at(place, chips):
    up = 2 * place
    down = 2 * (chips - 1 - place) + 1
    if isinstance(place, int):
        return up if place < chips // 2 else down
    return jnp.where(place < chips // 2, up, down)


def place_of(chip, chips):
    if isinstance(chip, int):
        return chip // 2 if chip % 2 == 0 else chips - 1 - chip // 2
    return jnp.where(chip % 2 == 0, chip // 2, chips - 1 - chip // 2)


def ring_pairs(chips):
    pairs = []
    for chip in range(chips):
        for core in range(CORES):
            step = 1 if core == 0 else -1
            target = chip_at((place_of(chip, chips) + step) % chips, chips)
            pairs.append((chip * CORES + core, target * CORES + core))
    return pairs


def swap_pairs(chips):
    return [(f, f ^ 1) for f in range(CORES * chips)]


def slots(chips):
    shared = []
    for step in range(1, chips // 2):
        shared += [(step, 0), (step, 1), (-step, 1), (-step, 0)]
    return shared + [(chips // 2, 0), (chips // 2, 1)], [(0, 0), (0, 1)]


def shard_of(slot, chips):
    back, other = slot
    me = lax.axis_index("fsdp")
    core = me % CORES
    direction = jnp.where(core == 0, -1, 1)
    place = (place_of(me // CORES, chips) + direction * back + chips) % chips
    return chip_at(place, chips) * CORES + (1 - core if other else core)


def cast_kernel(grad, out):
    out[...] = grad[...].astype(out.dtype)


def cast_half(grad, which):
    rows, cols = grad.shape
    half = rows // 2
    steps = 2
    tall = half // steps
    return pl.pallas_call(
        cast_kernel,
        grid=(steps,),
        in_specs=[pl.BlockSpec((tall, cols), lambda g: (which() * steps + g, 0))],
        out_specs=pl.BlockSpec((tall, cols), lambda g: (g, 0)),
        out_shape=jax.ShapeDtypeStruct((half, cols), jnp.bfloat16),
        compiler_params=params(),
        cost_estimate=pl.CostEstimate(flops=half * cols, bytes_accessed=6 * half * cols, transcendentals=0),
    )(grad)


def mine():
    return lax.axis_index("island")


def others():
    return 1 - lax.axis_index("island")


def tiles(shape, tall, wide):
    rows, cols = shape
    return [(slice(r, r + tall), slice(c, c + wide)) for r in range(0, rows, tall) for c in range(0, cols, wide)]


def token_kernel(chips, half, tokens, grad, own, sent, whole, inverse):
    rows, width = tokens.shape
    shared, kept = slots(chips)

    def columns(slot, which):
        start = shard_of(slot, chips) * 2 * half + which * half
        return tokens[:, pl.ds(pl.multiple_of(start, half), half)]

    for k, slot in enumerate(shared):
        own[k] = columns(slot, mine())
        sent[k] = columns(slot, others())
    for k, at in enumerate(tiles(grad.shape, rows, half)):
        sent[len(shared) + k] = grad[at]
    for k, slot in enumerate(kept):
        whole[2 * k] = columns(slot, mine())
        whole[2 * k + 1] = columns(slot, others())
    total = jnp.zeros((rows, BLOCK), jnp.float32)
    for k in range(width // BLOCK):
        part = tokens[:, k * BLOCK : (k + 1) * BLOCK].astype(jnp.float32)
        total += part * part
    mean = jnp.sum(total, axis=1, keepdims=True) / width
    inverse[...] = lax.rsqrt(mean + 1e-05) / jnp.sqrt(jnp.float32(width))


def split_tokens(tokens, grad, chips):
    rows, width = tokens.shape
    half = width // (chips * CORES * 2)
    shared, kept = slots(chips)
    counts = len(shared), len(shared) + len(tiles(grad.shape, rows, half)), 2 * len(kept)
    return pl.pallas_call(
        functools.partial(token_kernel, chips, half),
        in_specs=[VMEM] * 2,
        out_specs=[VMEM] * 4,
        out_shape=[jax.ShapeDtypeStruct((count, rows, half), tokens.dtype) for count in counts]
        + [jax.ShapeDtypeStruct((rows, 1), jnp.float32)],
        compiler_params=params(),
        cost_estimate=pl.CostEstimate(flops=2 * rows * width, bytes_accessed=4 * rows * width, transcendentals=0),
    )(tokens, grad)


def unpack_kernel(first, packed, grad):
    for k, at in enumerate(tiles(grad.shape, *packed.shape[1:])):
        grad[at] = packed[first + k]


def unpack(first, packed, shape):
    return pl.pallas_call(
        functools.partial(unpack_kernel, first),
        in_specs=[VMEM],
        out_specs=VMEM,
        out_shape=jax.ShapeDtypeStruct(shape, packed.dtype),
        compiler_params=params(),
        cost_estimate=pl.CostEstimate(flops=0, bytes_accessed=4 * shape[0] * shape[1], transcendentals=0),
    )(packed)


def synced(a, b):
    a, b = a.astype(jnp.float32), b.astype(jnp.float32)
    peak_a = jnp.max(jnp.abs(a), axis=1, keepdims=True)
    peak_b = jnp.max(jnp.abs(b), axis=1, keepdims=True)
    shared = (peak_a + peak_b) / 2 + 1e-06
    over = 1.0 / shared
    low_a = jnp.clip(a * over, -1.0, 1.0).astype(jnp.bfloat16).astype(jnp.float32)
    low_b = jnp.clip(b * over, -1.0, 1.0).astype(jnp.bfloat16).astype(jnp.float32)
    return shared * (low_a + low_b) / 2


def gains_of(gain, row):
    return jnp.transpose(jnp.broadcast_to(gain[pl.ds(row // BLOCK, 1), :], (BLOCK, BLOCK)))


def ready_kernel(own, master, momentum, gain, peaks, base, steep):
    half, cols = own.shape
    first = lax.axis_index("fsdp") * (2 * half)
    slope = -outer_rate * (1 + outer_mu)
    for start in range(0, half, BLOCK):
        rows = slice(start, start + BLOCK)
        there = mine() * half + start
        held = pl.ds(pl.multiple_of(there, BLOCK), BLOCK)
        gains = gains_of(gain, first + there)
        steep[rows, :] = gains * slope / 2
        for k, col in enumerate(range(0, cols, BLOCK)):
            at = slice(col, col + BLOCK)
            a = jnp.abs(own[rows, at].astype(jnp.float32))
            peaks[k, rows, :] = jnp.broadcast_to(jnp.max(a, axis=1, keepdims=True) / 2 + 1e-06, a.shape)
            base[rows, at] = gains * (master[held, at] - outer_rate * outer_mu * (outer_mu * momentum[held, at]))


def get_ready(own, master, momentum, gain):
    half, cols = own.shape
    shapes = (cols // BLOCK, half, BLOCK), (half, cols), (half, BLOCK)
    return pl.pallas_call(
        ready_kernel,
        in_specs=[VMEM] * 4,
        out_specs=[VMEM] * 3,
        out_shape=[jax.ShapeDtypeStruct(shape, jnp.float32) for shape in shapes],
        compiler_params=params(),
        cost_estimate=pl.CostEstimate(flops=8 * half * cols, bytes_accessed=18 * half * cols, transcendentals=0),
    )(own, master, momentum, gain)


def first_kernel(own, here, peaks, base, steep, weight):
    half, cols = own.shape
    for start in range(0, half, BLOCK):
        rows = slice(start, start + BLOCK)
        for k, col in enumerate(range(0, cols, BLOCK)):
            at = slice(col, col + BLOCK)
            a = own[rows, at].astype(jnp.float32)
            b = here[rows, at].astype(jnp.float32)
            shared = peaks[k, rows, :] + jnp.max(jnp.abs(b), axis=1, keepdims=True) / 2
            over = 1.0 / shared[:, :1]
            low_a = jnp.clip(a * over, -1.0, 1.0).astype(jnp.bfloat16).astype(jnp.float32)
            low_b = jnp.clip(b * over, -1.0, 1.0).astype(jnp.bfloat16).astype(jnp.float32)
            weight[rows, at] = (base[rows, at] + steep[rows, :] * shared * (low_a + low_b)).astype(weight.dtype)


def first_weight(own, here, ready):
    half, cols = own.shape
    return pl.pallas_call(
        first_kernel,
        in_specs=[VMEM] * 5,
        out_specs=VMEM,
        out_shape=jax.ShapeDtypeStruct((half, cols), jnp.bfloat16),
        compiler_params=params(),
        cost_estimate=pl.CostEstimate(flops=20 * half * cols, bytes_accessed=14 * half * cols, transcendentals=0),
    )(own, here, *ready)


def weight_kernel(which, first, second, master, momentum, gain, weight):
    half, cols = first.shape
    base = lax.axis_index("fsdp") * (2 * half)
    for start in range(0, half, BLOCK):
        rows = slice(start, start + BLOCK)
        there = which() * half + start
        held = pl.ds(pl.multiple_of(there, BLOCK), BLOCK)
        gains = gains_of(gain, base + there)
        for col in range(0, cols, BLOCK):
            at = slice(col, col + BLOCK)
            outer_grad = synced(first[rows, at], second[rows, at])
            moved = outer_mu * momentum[held, at] + outer_grad
            fresh = master[held, at] - outer_rate * (outer_grad + outer_mu * moved)
            weight[rows, at] = (gains * fresh).astype(weight.dtype)


def sync_weight(which, first, second, master, momentum, gain):
    half, cols = first.shape
    return pl.pallas_call(
        functools.partial(weight_kernel, which),
        in_specs=[VMEM] * 5,
        out_specs=VMEM,
        out_shape=jax.ShapeDtypeStruct((half, cols), jnp.bfloat16),
        compiler_params=params(),
        cost_estimate=pl.CostEstimate(
            flops=30 * half * cols, bytes_accessed=14 * half * cols, transcendentals=0
        ),
    )(first, second, master, momentum, gain)


def outer_kernel(here_a, here_b, there_a, there_b, master, momentum, master_new, momentum_new):
    half, cols = here_a.shape
    for which, a, b in ((mine(), here_a, here_b), (others(), there_a, there_b)):
        for start in range(0, half, BLOCK):
            rows = slice(start, start + BLOCK)
            held = pl.ds(pl.multiple_of(which * half + start, BLOCK), BLOCK)
            for col in range(0, cols, BLOCK):
                at = slice(col, col + BLOCK)
                outer_grad = synced(a[rows, at], b[rows, at])
                moved = outer_mu * momentum[held, at] + outer_grad
                momentum_new[held, at] = moved
                master_new[held, at] = master[held, at] - outer_rate * (outer_grad + outer_mu * moved)


def sync_outer(here_a, here_b, there_a, there_b, master, momentum):
    rows, cols = master.shape
    full = jax.ShapeDtypeStruct(master.shape, jnp.float32)
    return pl.pallas_call(
        outer_kernel,
        in_specs=[VMEM] * 6,
        out_specs=[VMEM] * 2,
        out_shape=[full, full],
        compiler_params=params(),
        cost_estimate=pl.CostEstimate(flops=30 * rows * cols, bytes_accessed=20 * rows * cols, transcendentals=0),
    )(here_a, here_b, there_a, there_b, master, momentum)


def cost_of(blocks, rows):
    depth, cols = blocks[0].shape
    count = len(blocks)
    return pl.CostEstimate(
        flops=2 * rows * cols * depth * count, bytes_accessed=2 * count * depth * (cols + rows), transcendentals=0
    )


def own_kernel(first, count, whole, *refs):
    blocks, out = refs[:count], refs[-1]
    total = refs[count][...] if len(refs) > count + 1 else jnp.zeros(out.shape, jnp.float32)
    for k, block in enumerate(blocks):
        total += jnp.dot(whole[first + k], block[...], preferred_element_type=jnp.float32)
    out[...] = total


def dot_own(first, whole, blocks, *total):
    return pl.pallas_call(
        functools.partial(own_kernel, first, len(blocks)),
        in_specs=[VMEM] * (1 + len(blocks) + len(total)),
        out_specs=VMEM,
        out_shape=jax.ShapeDtypeStruct((whole.shape[1], blocks[0].shape[1]), jnp.float32),
        compiler_params=params(),
        cost_estimate=cost_of(blocks, whole.shape[1]),
    )(whole, *blocks, *total)


def early_kernel(start, count, own, other, *refs):
    blocks, total = refs[:count], refs[-1]
    total[...] = refs[count][...] if len(refs) > count + 1 else jnp.zeros(total.shape, jnp.float32)
    for k, block in enumerate(blocks):
        left = jnp.concatenate([own[start + k], other[start + k]], axis=0)
        total[...] += jnp.dot(left, block[...], preferred_element_type=jnp.float32)


def dot_early(start, own, other, blocks, *total):
    shape = (2 * own.shape[1], blocks[0].shape[1])
    return pl.pallas_call(
        functools.partial(early_kernel, start, len(blocks)),
        in_specs=[VMEM] * (2 + len(blocks) + len(total)),
        out_specs=VMEM,
        out_shape=jax.ShapeDtypeStruct(shape, jnp.float32),
        compiler_params=params(),
        cost_estimate=cost_of(blocks, shape[0]),
    )(own, other, *blocks, *total)


def late_kernel(start, own, other, early, *refs):
    *blocks, mine_part, sent_part = refs
    rows = own.shape[1]
    total = early[...]
    for k, block in enumerate(blocks):
        left = jnp.concatenate([own[start + k], other[start + k]], axis=0)
        total += jnp.dot(left, block[...], preferred_element_type=jnp.float32)
    mine_part[...] = total[:rows]
    sent_part[...] = total[rows:].astype(sent_part.dtype)


def dot_late(start, own, other, early, blocks):
    shape = (own.shape[1], blocks[0].shape[1])
    return pl.pallas_call(
        functools.partial(late_kernel, start),
        in_specs=[VMEM] * (3 + len(blocks)),
        out_specs=[VMEM] * 2,
        out_shape=[jax.ShapeDtypeStruct(shape, jnp.float32), jax.ShapeDtypeStruct(shape, jnp.bfloat16)],
        compiler_params=params(),
        cost_estimate=cost_of(blocks, 2 * shape[0]),
    )(own, other, early, *blocks)


def close_kernel(own_part, mine_part, other_part, inverse, keys):
    total = own_part[...] + mine_part[...] + other_part[...].astype(jnp.float32)
    keys[...] = (total * inverse[...]).astype(keys.dtype)


def close(own_part, mine_part, other_part, inverse):
    return pl.pallas_call(
        close_kernel,
        in_specs=[VMEM] * 4,
        out_specs=VMEM,
        out_shape=jax.ShapeDtypeStruct(mine_part.shape, jnp.bfloat16),
        compiler_params=params(),
    )(own_part, mine_part, other_part, inverse)


def by_permutes(tokens, norm_gain, master, momentum, pseudo_grad):
    chips = lax.axis_size("fsdp") // CORES
    ring = functools.partial(lax.ppermute, axis_name="fsdp", perm=ring_pairs(chips))
    swap = functools.partial(lax.ppermute, axis_name="fsdp", perm=swap_pairs(chips))
    cross = functools.partial(lax.ppermute, axis_name="island", perm=[(0, 1), (1, 0)])
    tie = lax.optimization_barrier

    gain = norm_gain.reshape(-1, BLOCK)
    half = master.shape[0] // 2
    grad_sent = lax.dynamic_slice_in_dim(pseudo_grad[0], others() * half, half).astype(jnp.bfloat16)
    grad_here = cross(grad_sent)
    grad_own = cast_half(pseudo_grad[0], mine)
    own, sent, whole, inverse = split_tokens(tokens, grad_own, chips)
    ready = get_ready(grad_own, master, momentum, gain)
    grad_here, own, *ready = tie((grad_here, own, *ready))
    other = cross(sent)

    a = weight = first_weight(grad_own, grad_here, ready)
    b = near = swap(weight)
    blocks = []
    for step in range(1, chips // 2):
        a, b = ring(a), ring(b)
        blocks += [a, b, swap(a), swap(b)]
    a = ring(a)
    ahead = len(blocks) - 2 * CORES
    total = dot_early(0, own, other, blocks[:ahead])
    far, total = tie((a, total))
    late = [a, swap(far)]

    grad_there = unpack(len(slots(chips)[0]), other, grad_own.shape)
    weight_over = sync_weight(others, grad_sent, grad_there, master, momentum, gain)
    own_part = dot_own(0, whole, [weight, weight_over, near, swap(weight_over)])
    master_new, momentum_new = sync_outer(grad_own, grad_here, grad_sent, grad_there, master, momentum)
    total = dot_early(ahead, own, other, blocks[ahead:], total)
    mine_part, sent_part = dot_late(len(blocks), own, other, total, late)
    keys = close(own_part, mine_part, cross(sent_part), inverse)
    return (keys, master_new, momentum_new)


def by_gathers(tokens, norm_gain, master, momentum, pseudo_grad):
    islands = lax.axis_size("island")
    island_grad = pseudo_grad[0]
    row_total, col_total = island_grad.shape
    every_island = lax.all_gather(
        pseudo_grad.astype(jnp.bfloat16), "island", axis=0, tiled=True
    ).astype(pseudo_grad.dtype)
    grouped_all = every_island.reshape(islands, row_total, col_total // BLOCK, BLOCK)
    peaks_all = jnp.max(jnp.abs(grouped_all), axis=3)
    shared = jnp.sum(peaks_all, axis=0) / islands + 1e-06
    quantized_all = jnp.clip(grouped_all / shared[None, :, :, None], -1.0, 1.0).astype(jnp.bfloat16)
    summed = jnp.sum(quantized_all.astype(jnp.float32), axis=0)
    outer_grad = (shared[:, :, None] * summed / islands).reshape(row_total, col_total)
    momentum_new = outer_mu * momentum + outer_grad
    master_new = master - outer_rate * (outer_grad + outer_mu * momentum_new)
    weight = master_new.astype(jnp.bfloat16)
    features = tokens.astype(jnp.float32)
    inverse = lax.rsqrt(jnp.mean(features * features, axis=1, keepdims=True) + 1e-05)
    normed = (features * inverse * norm_gain[None, :]).astype(jnp.bfloat16)
    scale = 1.0 / jnp.sqrt(jnp.float32(normed.shape[1]))
    gathered = lax.all_gather(weight, "fsdp", axis=0, tiled=True)
    product = jnp.dot(normed, gathered, preferred_element_type=jnp.float32)
    keys = (product * scale).astype(jnp.bfloat16)
    return (keys, master_new, momentum_new)


def on_device(tokens, norm_gain, master, momentum, pseudo_grad):
    shards = lax.axis_size("fsdp")
    rows = master.shape[0]
    ringed = shards % (2 * CORES) == 0 and 4 * CORES <= shards <= RING_LIMIT * CORES
    tiled = tokens.shape[0] == BLOCK and rows % (2 * BLOCK) == 0 and 2 * master.shape[1] % rows == 0
    if lax.axis_size("island") == 2 and ringed and tiled:
        return by_permutes(tokens, norm_gain, master, momentum, pseudo_grad)
    return by_gathers(tokens, norm_gain, master, momentum, pseudo_grad)


def solution(mesh):
    placed = (
        P(("island", "fsdp"), None),
        P(),
        P("fsdp", None),
        P("fsdp", None),
        P("island", "fsdp", None),
    )
    return jax.shard_map(
        on_device,
        mesh=mesh,
        in_specs=placed,
        out_specs=(P(("island", "fsdp"), None), P("fsdp", None), P("fsdp", None)),
        check_vma=False,
    )
```

```python
import functools

import jax
import jax.numpy as jnp
from jax import lax
from jax.experimental import pallas as pl
from jax.experimental.pallas import tpu as pltpu
from jax.sharding import PartitionSpec as P

BLOCK = 128
CORES = 2
RING_LIMIT = 16
PACKED = 2
COPIES = 2

outer_rate = 0.7
outer_mu = 0.9
VMEM = pl.BlockSpec(memory_space=pltpu.VMEM)
VMEM_LIMIT = 40 * 1024 * 1024


def params():
    return pltpu.CompilerParams(vmem_limit_bytes=VMEM_LIMIT)


def chip_at(place, chips):
    up = 2 * place
    down = 2 * (chips - 1 - place) + 1
    if isinstance(place, int):
        return up if place < chips // 2 else down
    return jnp.where(place < chips // 2, up, down)


def place_of(chip, chips):
    if isinstance(chip, int):
        return chip // 2 if chip % 2 == 0 else chips - 1 - chip // 2
    return jnp.where(chip % 2 == 0, chip // 2, chips - 1 - chip // 2)


def ring_pairs(chips):
    pairs = []
    for chip in range(chips):
        for core in range(CORES):
            step = 1 if core == 0 else -1
            target = chip_at((place_of(chip, chips) + step) % chips, chips)
            pairs.append((chip * CORES + core, target * CORES + core))
    return pairs


def swap_pairs(chips):
    return [(f, f ^ 1) for f in range(CORES * chips)]


def slots(chips):
    shared = []
    for step in range(1, chips // 2):
        shared += [(step, 0), (step, 1), (-step, 1), (-step, 0)]
    return shared + [(chips // 2, 0), (chips // 2, 1)], [(0, 0), (0, 1)]


def shard_of(slot, chips):
    back, other = slot
    me = lax.axis_index("fsdp")
    core = me % CORES
    direction = jnp.where(core == 0, -1, 1)
    place = (place_of(me // CORES, chips) + direction * back + chips) % chips
    return chip_at(place, chips) * CORES + (1 - core if other else core)


def cast_kernel(grad, *outs):
    start = 0
    for out in outs:
        out[...] = grad[start : start + out.shape[0]].astype(out.dtype)
        start += out.shape[0]


def cast_half(grad, which, *heights):
    rows, cols = grad.shape
    half = rows // 2
    return pl.pallas_call(
        cast_kernel,
        grid=(1,),
        in_specs=[pl.BlockSpec((half, cols), lambda g: (which(), 0))],
        out_specs=[pl.BlockSpec((height, cols), lambda g: (0, 0)) for height in heights],
        out_shape=[jax.ShapeDtypeStruct((height, cols), jnp.bfloat16) for height in heights],
        compiler_params=params(),
        cost_estimate=pl.CostEstimate(flops=half * cols, bytes_accessed=6 * half * cols, transcendentals=0),
    )(grad)


def join_kernel(*refs):
    *parts, out = refs
    start = 0
    for part in parts:
        out[start : start + part.shape[0]] = part[...]
        start += part.shape[0]


def join(*parts):
    rows, cols = sum(part.shape[0] for part in parts), parts[0].shape[1]
    return pl.pallas_call(
        join_kernel,
        in_specs=[VMEM] * len(parts),
        out_specs=VMEM,
        out_shape=jax.ShapeDtypeStruct((rows, cols), parts[0].dtype),
        compiler_params=params(),
        cost_estimate=pl.CostEstimate(flops=0, bytes_accessed=4 * rows * cols, transcendentals=0),
    )(*parts)


def mine():
    return lax.axis_index("island")


def others():
    return 1 - lax.axis_index("island")


def tiles(shape, tall, wide):
    rows, cols = shape
    return [(slice(r, r + tall), slice(c, c + wide)) for r in range(0, rows, tall) for c in range(0, cols, wide)]


def token_kernel(chips, half, tokens, grad, own, sent, more, whole, inverse):
    rows, width = tokens.shape
    shared, kept = slots(chips)

    def columns(slot, which):
        start = shard_of(slot, chips) * 2 * half + which * half
        return tokens[:, pl.ds(pl.multiple_of(start, half), half)]

    for k, slot in enumerate(shared):
        own[k] = columns(slot, mine())
        sent[k] = columns(slot, others())
    for k, at in enumerate(tiles(grad.shape, rows, half)):
        if k < PACKED:
            sent[len(shared) + k] = grad[at]
        else:
            more[k - PACKED] = grad[at]
    for k, slot in enumerate(kept):
        whole[2 * k] = columns(slot, mine())
        whole[2 * k + 1] = columns(slot, others())
    total = jnp.zeros((rows, BLOCK), jnp.float32)
    for k in range(width // BLOCK):
        part = tokens[:, k * BLOCK : (k + 1) * BLOCK].astype(jnp.float32)
        total += part * part
    mean = jnp.sum(total, axis=1, keepdims=True) / width
    inverse[...] = lax.rsqrt(mean + 1e-05) / jnp.sqrt(jnp.float32(width))


def split_tokens(tokens, grad, chips):
    rows, width = tokens.shape
    half = width // (chips * CORES * 2)
    shared, kept = slots(chips)
    count = len(tiles(grad.shape, rows, half))
    counts = len(shared), len(shared) + PACKED, count - PACKED, 2 * len(kept)
    return pl.pallas_call(
        functools.partial(token_kernel, chips, half),
        in_specs=[VMEM] * 2,
        out_specs=[VMEM] * 5,
        out_shape=[jax.ShapeDtypeStruct((count, rows, half), tokens.dtype) for count in counts]
        + [jax.ShapeDtypeStruct((rows, 1), jnp.float32)],
        compiler_params=params(),
        cost_estimate=pl.CostEstimate(flops=2 * rows * width, bytes_accessed=4 * rows * width, transcendentals=0),
    )(tokens, grad)


def unpack_kernel(first, packed, more, grad):
    count = packed.shape[0] - first
    for k, at in enumerate(tiles(grad.shape, *packed.shape[1:])):
        grad[at] = packed[first + k] if k < count else more[k - count]


def unpack(first, packed, more, shape):
    return pl.pallas_call(
        functools.partial(unpack_kernel, first),
        in_specs=[VMEM] * 2,
        out_specs=VMEM,
        out_shape=jax.ShapeDtypeStruct(shape, packed.dtype),
        compiler_params=params(),
        cost_estimate=pl.CostEstimate(flops=0, bytes_accessed=4 * shape[0] * shape[1], transcendentals=0),
    )(packed, more)


def synced(a, b):
    a, b = a.astype(jnp.float32), b.astype(jnp.float32)
    peak_a = jnp.max(jnp.abs(a), axis=1, keepdims=True)
    peak_b = jnp.max(jnp.abs(b), axis=1, keepdims=True)
    shared = (peak_a + peak_b) / 2 + 1e-06
    over = 1.0 / shared
    low_a = jnp.clip(a * over, -1.0, 1.0).astype(jnp.bfloat16).astype(jnp.float32)
    low_b = jnp.clip(b * over, -1.0, 1.0).astype(jnp.bfloat16).astype(jnp.float32)
    return shared * (low_a + low_b) / 2


def gains_of(gain, row):
    return jnp.transpose(jnp.broadcast_to(gain[pl.ds(row // BLOCK, 1), :], (BLOCK, BLOCK)))


def ready_kernel(own, master, momentum, gain, peaks, base, steep):
    half, cols = own.shape
    first = lax.axis_index("fsdp") * (2 * half)
    slope = -outer_rate * (1 + outer_mu)
    for start in range(0, half, BLOCK):
        rows = slice(start, start + BLOCK)
        there = mine() * half + start
        held = pl.ds(pl.multiple_of(there, BLOCK), BLOCK)
        gains = gains_of(gain, first + there)
        steep[rows, :] = gains * slope / 2
        for k, col in enumerate(range(0, cols, BLOCK)):
            at = slice(col, col + BLOCK)
            a = jnp.abs(own[rows, at].astype(jnp.float32))
            peaks[k, rows, :] = jnp.broadcast_to(jnp.max(a, axis=1, keepdims=True) / 2 + 1e-06, a.shape)
            base[rows, at] = gains * (master[held, at] - outer_rate * outer_mu * (outer_mu * momentum[held, at]))


def get_ready(own, master, momentum, gain):
    half, cols = own.shape
    shapes = (cols // BLOCK, half, BLOCK), (half, cols), (half, BLOCK)
    return pl.pallas_call(
        ready_kernel,
        in_specs=[VMEM] * 4,
        out_specs=[VMEM] * 3,
        out_shape=[jax.ShapeDtypeStruct(shape, jnp.float32) for shape in shapes],
        compiler_params=params(),
        cost_estimate=pl.CostEstimate(flops=8 * half * cols, bytes_accessed=18 * half * cols, transcendentals=0),
    )(own, master, momentum, gain)


def first_part(offset, own, here, peaks, base, steep, weight):
    rows = slice(offset, offset + here.shape[0])
    for k, col in enumerate(range(0, own.shape[1], BLOCK)):
        at = slice(col, col + BLOCK)
        a = own[rows, at].astype(jnp.float32)
        b = here[:, at].astype(jnp.float32)
        shared = peaks[k, rows, :] + jnp.max(jnp.abs(b), axis=1, keepdims=True) / 2
        over = 1.0 / shared[:, :1]
        low_a = jnp.clip(a * over, -1.0, 1.0).astype(jnp.bfloat16).astype(jnp.float32)
        low_b = jnp.clip(b * over, -1.0, 1.0).astype(jnp.bfloat16).astype(jnp.float32)
        weight[:, at] = (base[rows, at] + steep[rows, :] * shared * (low_a + low_b)).astype(weight.dtype)


def first_kernel(own, here, peaks, base, steep, weight):
    first_part(0, own, here, peaks, base, steep, weight)


def second_kernel(own, here, peaks, base, steep, done, weight, whole):
    offset = done.shape[0]
    first_part(offset, own, here, peaks, base, steep, weight)
    whole[:offset] = done[...]
    whole[offset:] = weight[...]


def half_weight(own, here, ready, *done):
    rows, cols = here.shape
    shapes = [(rows, cols)] + [(part.shape[0] + rows, cols) for part in done]
    return pl.pallas_call(
        second_kernel if done else first_kernel,
        in_specs=[VMEM] * (5 + len(done)),
        out_specs=[VMEM] * len(shapes),
        out_shape=[jax.ShapeDtypeStruct(shape, jnp.bfloat16) for shape in shapes],
        compiler_params=params(),
        cost_estimate=pl.CostEstimate(flops=20 * rows * cols, bytes_accessed=14 * rows * cols, transcendentals=0),
    )(own, here, *ready, *done)


def weight_kernel(which, first, second, master, momentum, gain, weight):
    half, cols = first.shape
    base = lax.axis_index("fsdp") * (2 * half)
    for start in range(0, half, BLOCK):
        rows = slice(start, start + BLOCK)
        there = which() * half + start
        held = pl.ds(pl.multiple_of(there, BLOCK), BLOCK)
        gains = gains_of(gain, base + there)
        for col in range(0, cols, BLOCK):
            at = slice(col, col + BLOCK)
            outer_grad = synced(first[rows, at], second[rows, at])
            moved = outer_mu * momentum[held, at] + outer_grad
            fresh = master[held, at] - outer_rate * (outer_grad + outer_mu * moved)
            weight[rows, at] = (gains * fresh).astype(weight.dtype)


def sync_weight(which, first, second, master, momentum, gain):
    half, cols = first.shape
    return pl.pallas_call(
        functools.partial(weight_kernel, which),
        in_specs=[VMEM] * 5,
        out_specs=VMEM,
        out_shape=jax.ShapeDtypeStruct((half, cols), jnp.bfloat16),
        compiler_params=params(),
        cost_estimate=pl.CostEstimate(
            flops=30 * half * cols, bytes_accessed=14 * half * cols, transcendentals=0
        ),
    )(first, second, master, momentum, gain)


def outer_kernel(here_a, here_b, there_a, there_b, master, momentum, master_new, momentum_new):
    half, cols = here_a.shape
    for which, a, b in ((mine(), here_a, here_b), (others(), there_a, there_b)):
        for start in range(0, half, BLOCK):
            rows = slice(start, start + BLOCK)
            held = pl.ds(pl.multiple_of(which * half + start, BLOCK), BLOCK)
            for col in range(0, cols, BLOCK):
                at = slice(col, col + BLOCK)
                outer_grad = synced(a[rows, at], b[rows, at])
                moved = outer_mu * momentum[held, at] + outer_grad
                momentum_new[held, at] = moved
                master_new[held, at] = master[held, at] - outer_rate * (outer_grad + outer_mu * moved)


def sync_outer(here_a, here_b, there_a, there_b, master, momentum):
    rows, cols = master.shape
    full = jax.ShapeDtypeStruct(master.shape, jnp.float32)
    return pl.pallas_call(
        outer_kernel,
        in_specs=[VMEM] * 6,
        out_specs=[VMEM] * 2,
        out_shape=[full, full],
        compiler_params=params(),
        cost_estimate=pl.CostEstimate(flops=30 * rows * cols, bytes_accessed=20 * rows * cols, transcendentals=0),
    )(here_a, here_b, there_a, there_b, master, momentum)


def cost_of(blocks, rows):
    depth, cols = blocks[0].shape
    count = len(blocks)
    return pl.CostEstimate(
        flops=2 * rows * cols * depth * count, bytes_accessed=2 * count * depth * (cols + rows), transcendentals=0
    )


def own_kernel(first, count, whole, *refs):
    blocks, out = refs[:count], refs[-1]
    total = refs[count][...] if len(refs) > count + 1 else jnp.zeros(out.shape, jnp.float32)
    for k, block in enumerate(blocks):
        total += jnp.dot(whole[first + k], block[...], preferred_element_type=jnp.float32)
    out[...] = total


def dot_own(first, whole, blocks, *total):
    return pl.pallas_call(
        functools.partial(own_kernel, first, len(blocks)),
        in_specs=[VMEM] * (1 + len(blocks) + len(total)),
        out_specs=VMEM,
        out_shape=jax.ShapeDtypeStruct((whole.shape[1], blocks[0].shape[1]), jnp.float32),
        compiler_params=params(),
        cost_estimate=cost_of(blocks, whole.shape[1]),
    )(whole, *blocks, *total)


def early_kernel(start, count, own, other, *refs):
    blocks, total = refs[:count], refs[-1]
    total[...] = refs[count][...] if len(refs) > count + 1 else jnp.zeros(total.shape, jnp.float32)
    for k, block in enumerate(blocks):
        left = jnp.concatenate([own[start + k], other[start + k]], axis=0)
        total[...] += jnp.dot(left, block[...], preferred_element_type=jnp.float32)


def dot_early(start, own, other, blocks, *total):
    shape = (2 * own.shape[1], blocks[0].shape[1])
    return pl.pallas_call(
        functools.partial(early_kernel, start, len(blocks)),
        in_specs=[VMEM] * (2 + len(blocks) + len(total)),
        out_specs=VMEM,
        out_shape=jax.ShapeDtypeStruct(shape, jnp.float32),
        compiler_params=params(),
        cost_estimate=cost_of(blocks, shape[0]),
    )(own, other, *blocks, *total)


def late_kernel(start, own, other, early, *refs):
    *blocks, mine_part, sent_part = refs
    rows = own.shape[1]
    total = early[...]
    for k, block in enumerate(blocks):
        left = jnp.concatenate([own[start + k], other[start + k]], axis=0)
        total += jnp.dot(left, block[...], preferred_element_type=jnp.float32)
    mine_part[...] = total[:rows]
    sent_part[...] = total[rows:].astype(sent_part.dtype)


def dot_late(start, own, other, early, blocks):
    shape = (own.shape[1], blocks[0].shape[1])
    return pl.pallas_call(
        functools.partial(late_kernel, start),
        in_specs=[VMEM] * (3 + len(blocks)),
        out_specs=[VMEM] * 2,
        out_shape=[jax.ShapeDtypeStruct(shape, jnp.float32), jax.ShapeDtypeStruct(shape, jnp.bfloat16)],
        compiler_params=params(),
        cost_estimate=cost_of(blocks, 2 * shape[0]),
    )(own, other, early, *blocks)


def close_kernel(own_part, mine_part, other_part, inverse, keys):
    total = own_part[...] + mine_part[...] + other_part[...].astype(jnp.float32)
    keys[...] = (total * inverse[...]).astype(keys.dtype)


def close(own_part, mine_part, other_part, inverse):
    return pl.pallas_call(
        close_kernel,
        in_specs=[VMEM] * 4,
        out_specs=VMEM,
        out_shape=jax.ShapeDtypeStruct(mine_part.shape, jnp.bfloat16),
        compiler_params=params(),
    )(own_part, mine_part, other_part, inverse)


def by_permutes(tokens, norm_gain, master, momentum, pseudo_grad):
    chips = lax.axis_size("fsdp") // CORES
    ring = functools.partial(lax.ppermute, axis_name="fsdp", perm=ring_pairs(chips))
    swap = functools.partial(lax.ppermute, axis_name="fsdp", perm=swap_pairs(chips))
    cross = functools.partial(lax.ppermute, axis_name="island", perm=[(0, 1), (1, 0)])
    tie = lax.optimization_barrier

    gain = norm_gain.reshape(-1, BLOCK)
    half = master.shape[0] // 2
    sent_parts = cast_half(pseudo_grad[0], others, half // 2, half // 2)
    here_parts = [cross(part) for part in sent_parts]
    (grad_own,) = cast_half(pseudo_grad[0], mine, half)
    own, sent, more, whole, inverse = split_tokens(tokens, grad_own, chips)
    ready = get_ready(grad_own, master, momentum, gain)
    here_parts[0], own, *ready = tie((here_parts[0], own, *ready))
    other, more = cross(sent), cross(more)

    (head,) = half_weight(grad_own, here_parts[0], ready)
    tail, weight = half_weight(grad_own, here_parts[1], ready, head)
    swapped = swap(head)
    for _ in range(COPIES):
        swapped = join(swapped)
    b = near = join(swapped, swap(tail))
    blocks = []
    for step in range(1, chips // 2):
        if step == 1:
            arrived = ring(head)
            for _ in range(COPIES):
                arrived = join(arrived)
            a = join(arrived, ring(tail))
        else:
            a = ring(a)
        b = ring(b)
        blocks += [a, b, swap(a), swap(b)]
    a = ring(a)
    ahead = len(blocks) - 2 * CORES
    total = dot_early(0, own, other, blocks[:ahead])
    far, total = tie((a, total))
    late = [a, swap(far)]

    grad_sent, grad_here = join(*sent_parts), join(*here_parts)
    grad_there = unpack(len(slots(chips)[0]), other, more, grad_own.shape)
    weight_over = sync_weight(others, grad_sent, grad_there, master, momentum, gain)
    own_part = dot_own(0, whole, [weight, weight_over, near, swap(weight_over)])
    master_new, momentum_new = sync_outer(grad_own, grad_here, grad_sent, grad_there, master, momentum)
    total = dot_early(ahead, own, other, blocks[ahead:], total)
    mine_part, sent_part = dot_late(len(blocks), own, other, total, late)
    keys = close(own_part, mine_part, cross(sent_part), inverse)
    return (keys, master_new, momentum_new)


def by_gathers(tokens, norm_gain, master, momentum, pseudo_grad):
    islands = lax.axis_size("island")
    island_grad = pseudo_grad[0]
    row_total, col_total = island_grad.shape
    every_island = lax.all_gather(
        pseudo_grad.astype(jnp.bfloat16), "island", axis=0, tiled=True
    ).astype(pseudo_grad.dtype)
    grouped_all = every_island.reshape(islands, row_total, col_total // BLOCK, BLOCK)
    peaks_all = jnp.max(jnp.abs(grouped_all), axis=3)
    shared = jnp.sum(peaks_all, axis=0) / islands + 1e-06
    quantized_all = jnp.clip(grouped_all / shared[None, :, :, None], -1.0, 1.0).astype(jnp.bfloat16)
    summed = jnp.sum(quantized_all.astype(jnp.float32), axis=0)
    outer_grad = (shared[:, :, None] * summed / islands).reshape(row_total, col_total)
    momentum_new = outer_mu * momentum + outer_grad
    master_new = master - outer_rate * (outer_grad + outer_mu * momentum_new)
    weight = master_new.astype(jnp.bfloat16)
    features = tokens.astype(jnp.float32)
    inverse = lax.rsqrt(jnp.mean(features * features, axis=1, keepdims=True) + 1e-05)
    normed = (features * inverse * norm_gain[None, :]).astype(jnp.bfloat16)
    scale = 1.0 / jnp.sqrt(jnp.float32(normed.shape[1]))
    gathered = lax.all_gather(weight, "fsdp", axis=0, tiled=True)
    product = jnp.dot(normed, gathered, preferred_element_type=jnp.float32)
    keys = (product * scale).astype(jnp.bfloat16)
    return (keys, master_new, momentum_new)


def on_device(tokens, norm_gain, master, momentum, pseudo_grad):
    shards = lax.axis_size("fsdp")
    rows = master.shape[0]
    ringed = shards % (2 * CORES) == 0 and 4 * CORES <= shards <= RING_LIMIT * CORES
    tiled = tokens.shape[0] == BLOCK and rows % (2 * BLOCK) == 0 and 2 * master.shape[1] % rows == 0
    if lax.axis_size("island") == 2 and ringed and tiled:
        return by_permutes(tokens, norm_gain, master, momentum, pseudo_grad)
    return by_gathers(tokens, norm_gain, master, momentum, pseudo_grad)


def solution(mesh):
    placed = (
        P(("island", "fsdp"), None),
        P(),
        P("fsdp", None),
        P("fsdp", None),
        P("island", "fsdp", None),
    )
    return jax.shard_map(
        on_device,
        mesh=mesh,
        in_specs=placed,
        out_specs=(P(("island", "fsdp"), None), P("fsdp", None), P("fsdp", None)),
        check_vma=False,
    )
```

```python
import functools

import jax
import jax.numpy as jnp
from jax import lax
from jax.experimental import pallas as pl
from jax.experimental.pallas import tpu as pltpu
from jax.sharding import PartitionSpec as P

BLOCK = 128
CORES = 2
RING_LIMIT = 16
PACKED = 2
COPIES = 2

outer_rate = 0.7
outer_mu = 0.9
VMEM = pl.BlockSpec(memory_space=pltpu.VMEM)
VMEM_LIMIT = 40 * 1024 * 1024


def params():
    return pltpu.CompilerParams(vmem_limit_bytes=VMEM_LIMIT)


def chip_at(place, chips):
    up = 2 * place
    down = 2 * (chips - 1 - place) + 1
    if isinstance(place, int):
        return up if place < chips // 2 else down
    return jnp.where(place < chips // 2, up, down)


def place_of(chip, chips):
    if isinstance(chip, int):
        return chip // 2 if chip % 2 == 0 else chips - 1 - chip // 2
    return jnp.where(chip % 2 == 0, chip // 2, chips - 1 - chip // 2)


def ring_pairs(chips):
    pairs = []
    for chip in range(chips):
        for core in range(CORES):
            step = 1 if core == 0 else -1
            target = chip_at((place_of(chip, chips) + step) % chips, chips)
            pairs.append((chip * CORES + core, target * CORES + core))
    return pairs


def swap_pairs(chips):
    return [(f, f ^ 1) for f in range(CORES * chips)]


def slots(chips):
    shared = []
    for step in range(1, chips // 2):
        shared += [(step, 0), (step, 1), (-step, 1), (-step, 0)]
    return shared + [(chips // 2, 0), (chips // 2, 1)], [(0, 0), (0, 1)]


def shard_of(slot, chips):
    back, other = slot
    me = lax.axis_index("fsdp")
    core = me % CORES
    direction = jnp.where(core == 0, -1, 1)
    place = (place_of(me // CORES, chips) + direction * back + chips) % chips
    return chip_at(place, chips) * CORES + (1 - core if other else core)


def cast_kernel(grad, *outs):
    start = 0
    for out in outs:
        out[...] = grad[start : start + out.shape[0]].astype(out.dtype)
        start += out.shape[0]


def cast_half(grad, which, *heights):
    rows, cols = grad.shape
    half = rows // 2
    return pl.pallas_call(
        cast_kernel,
        grid=(1,),
        in_specs=[pl.BlockSpec((half, cols), lambda g: (which(), 0))],
        out_specs=[pl.BlockSpec((height, cols), lambda g: (0, 0)) for height in heights],
        out_shape=[jax.ShapeDtypeStruct((height, cols), jnp.bfloat16) for height in heights],
        compiler_params=params(),
        cost_estimate=pl.CostEstimate(flops=half * cols, bytes_accessed=6 * half * cols, transcendentals=0),
    )(grad)


def join_kernel(*refs):
    *parts, out = refs
    start = 0
    for part in parts:
        out[start : start + part.shape[0]] = part[...]
        start += part.shape[0]


def join(*parts):
    rows, cols = sum(part.shape[0] for part in parts), parts[0].shape[1]
    return pl.pallas_call(
        join_kernel,
        in_specs=[VMEM] * len(parts),
        out_specs=VMEM,
        out_shape=jax.ShapeDtypeStruct((rows, cols), parts[0].dtype),
        compiler_params=params(),
        cost_estimate=pl.CostEstimate(flops=0, bytes_accessed=4 * rows * cols, transcendentals=0),
    )(*parts)


def mine():
    return lax.axis_index("island")


def others():
    return 1 - lax.axis_index("island")


def tiles(shape, tall, wide):
    rows, cols = shape
    return [(slice(r, r + tall), slice(c, c + wide)) for r in range(0, rows, tall) for c in range(0, cols, wide)]


def token_kernel(chips, half, tokens, grad, own, sent, more, whole, inverse):
    rows, width = tokens.shape
    shared, kept = slots(chips)

    def columns(slot, which):
        start = shard_of(slot, chips) * 2 * half + which * half
        return tokens[:, pl.ds(pl.multiple_of(start, half), half)]

    for k, slot in enumerate(shared):
        own[k] = columns(slot, mine())
        sent[k] = columns(slot, others())
    for k, at in enumerate(tiles(grad.shape, rows, half)):
        if k < PACKED:
            sent[len(shared) + k] = grad[at]
        else:
            more[k - PACKED] = grad[at]
    for k, slot in enumerate(kept):
        whole[2 * k] = columns(slot, mine())
        whole[2 * k + 1] = columns(slot, others())
    total = jnp.zeros((rows, BLOCK), jnp.float32)
    for k in range(width // BLOCK):
        part = tokens[:, k * BLOCK : (k + 1) * BLOCK].astype(jnp.float32)
        total += part * part
    mean = jnp.sum(total, axis=1, keepdims=True) / width
    inverse[...] = lax.rsqrt(mean + 1e-05) / jnp.sqrt(jnp.float32(width))


def split_tokens(tokens, grad, chips):
    rows, width = tokens.shape
    half = width // (chips * CORES * 2)
    shared, kept = slots(chips)
    count = len(tiles(grad.shape, rows, half))
    counts = len(shared), len(shared) + PACKED, count - PACKED, 2 * len(kept)
    return pl.pallas_call(
        functools.partial(token_kernel, chips, half),
        in_specs=[VMEM] * 2,
        out_specs=[VMEM] * 5,
        out_shape=[jax.ShapeDtypeStruct((count, rows, half), tokens.dtype) for count in counts]
        + [jax.ShapeDtypeStruct((rows, 1), jnp.float32)],
        compiler_params=params(),
        cost_estimate=pl.CostEstimate(flops=2 * rows * width, bytes_accessed=4 * rows * width, transcendentals=0),
    )(tokens, grad)


def unpack_kernel(first, packed, more, grad):
    count = packed.shape[0] - first
    for k, at in enumerate(tiles(grad.shape, *packed.shape[1:])):
        grad[at] = packed[first + k] if k < count else more[k - count]


def unpack(first, packed, more, shape):
    return pl.pallas_call(
        functools.partial(unpack_kernel, first),
        in_specs=[VMEM] * 2,
        out_specs=VMEM,
        out_shape=jax.ShapeDtypeStruct(shape, packed.dtype),
        compiler_params=params(),
        cost_estimate=pl.CostEstimate(flops=0, bytes_accessed=4 * shape[0] * shape[1], transcendentals=0),
    )(packed, more)


def synced(a, b):
    a, b = a.astype(jnp.float32), b.astype(jnp.float32)
    peak_a = jnp.max(jnp.abs(a), axis=1, keepdims=True)
    peak_b = jnp.max(jnp.abs(b), axis=1, keepdims=True)
    shared = (peak_a + peak_b) / 2 + 1e-06
    over = 1.0 / shared
    low_a = jnp.clip(a * over, -1.0, 1.0).astype(jnp.bfloat16).astype(jnp.float32)
    low_b = jnp.clip(b * over, -1.0, 1.0).astype(jnp.bfloat16).astype(jnp.float32)
    return shared * (low_a + low_b) / 2


def gains_of(gain, row):
    return jnp.transpose(jnp.broadcast_to(gain[pl.ds(row // BLOCK, 1), :], (BLOCK, BLOCK)))


def ready_kernel(own, master, momentum, gain, peaks, base, steep):
    half, cols = own.shape
    first = lax.axis_index("fsdp") * (2 * half)
    slope = -outer_rate * (1 + outer_mu)
    for start in range(0, half, BLOCK):
        rows = slice(start, start + BLOCK)
        there = mine() * half + start
        held = pl.ds(pl.multiple_of(there, BLOCK), BLOCK)
        gains = gains_of(gain, first + there)
        steep[rows, :] = gains * slope / 2
        for k, col in enumerate(range(0, cols, BLOCK)):
            at = slice(col, col + BLOCK)
            a = jnp.abs(own[rows, at].astype(jnp.float32))
            peaks[k, rows, :] = jnp.broadcast_to(jnp.max(a, axis=1, keepdims=True) / 2 + 1e-06, a.shape)
            base[rows, at] = gains * (master[held, at] - outer_rate * outer_mu * (outer_mu * momentum[held, at]))


def get_ready(own, master, momentum, gain):
    half, cols = own.shape
    shapes = (cols // BLOCK, half, BLOCK), (half, cols), (half, BLOCK)
    return pl.pallas_call(
        ready_kernel,
        in_specs=[VMEM] * 4,
        out_specs=[VMEM] * 3,
        out_shape=[jax.ShapeDtypeStruct(shape, jnp.float32) for shape in shapes],
        compiler_params=params(),
        cost_estimate=pl.CostEstimate(flops=8 * half * cols, bytes_accessed=18 * half * cols, transcendentals=0),
    )(own, master, momentum, gain)


def first_part(offset, own, here, peaks, base, steep, weight):
    rows = slice(offset, offset + here.shape[0])
    for k, col in enumerate(range(0, own.shape[1], BLOCK)):
        at = slice(col, col + BLOCK)
        a = own[rows, at].astype(jnp.float32)
        b = here[:, at].astype(jnp.float32)
        shared = peaks[k, rows, :] + jnp.max(jnp.abs(b), axis=1, keepdims=True) / 2
        over = 1.0 / shared
        low_a = jnp.clip(a * over, -1.0, 1.0).astype(jnp.bfloat16).astype(jnp.float32)
        low_b = jnp.clip(b * over, -1.0, 1.0).astype(jnp.bfloat16).astype(jnp.float32)
        weight[:, at] = (base[rows, at] + steep[rows, :] * shared * (low_a + low_b)).astype(weight.dtype)


def first_kernel(own, here, peaks, base, steep, weight):
    first_part(0, own, here, peaks, base, steep, weight)


def second_kernel(own, here, peaks, base, steep, done, weight, whole):
    offset = done.shape[0]
    first_part(offset, own, here, peaks, base, steep, weight)
    whole[:offset] = done[...]
    whole[offset:] = weight[...]


def half_weight(own, here, ready, *done):
    rows, cols = here.shape
    shapes = [(rows, cols)] + [(part.shape[0] + rows, cols) for part in done]
    return pl.pallas_call(
        second_kernel if done else first_kernel,
        in_specs=[VMEM] * (5 + len(done)),
        out_specs=[VMEM] * len(shapes),
        out_shape=[jax.ShapeDtypeStruct(shape, jnp.bfloat16) for shape in shapes],
        compiler_params=params(),
        cost_estimate=pl.CostEstimate(flops=20 * rows * cols, bytes_accessed=14 * rows * cols, transcendentals=0),
    )(own, here, *ready, *done)


def weight_kernel(which, first, second, master, momentum, gain, weight):
    half, cols = first.shape
    base = lax.axis_index("fsdp") * (2 * half)
    for start in range(0, half, BLOCK):
        rows = slice(start, start + BLOCK)
        there = which() * half + start
        held = pl.ds(pl.multiple_of(there, BLOCK), BLOCK)
        gains = gains_of(gain, base + there)
        for col in range(0, cols, BLOCK):
            at = slice(col, col + BLOCK)
            outer_grad = synced(first[rows, at], second[rows, at])
            moved = outer_mu * momentum[held, at] + outer_grad
            fresh = master[held, at] - outer_rate * (outer_grad + outer_mu * moved)
            weight[rows, at] = (gains * fresh).astype(weight.dtype)


def sync_weight(which, first, second, master, momentum, gain):
    half, cols = first.shape
    return pl.pallas_call(
        functools.partial(weight_kernel, which),
        in_specs=[VMEM] * 5,
        out_specs=VMEM,
        out_shape=jax.ShapeDtypeStruct((half, cols), jnp.bfloat16),
        compiler_params=params(),
        cost_estimate=pl.CostEstimate(
            flops=30 * half * cols, bytes_accessed=14 * half * cols, transcendentals=0
        ),
    )(first, second, master, momentum, gain)


def outer_kernel(here_a, here_b, there_a, there_b, master, momentum, master_new, momentum_new):
    half, cols = here_a.shape
    for which, a, b in ((mine(), here_a, here_b), (others(), there_a, there_b)):
        for start in range(0, half, BLOCK):
            rows = slice(start, start + BLOCK)
            held = pl.ds(pl.multiple_of(which * half + start, BLOCK), BLOCK)
            for col in range(0, cols, BLOCK):
                at = slice(col, col + BLOCK)
                outer_grad = synced(a[rows, at], b[rows, at])
                moved = outer_mu * momentum[held, at] + outer_grad
                momentum_new[held, at] = moved
                master_new[held, at] = master[held, at] - outer_rate * (outer_grad + outer_mu * moved)


def sync_outer(here_a, here_b, there_a, there_b, master, momentum):
    rows, cols = master.shape
    full = jax.ShapeDtypeStruct(master.shape, jnp.float32)
    return pl.pallas_call(
        outer_kernel,
        in_specs=[VMEM] * 6,
        out_specs=[VMEM] * 2,
        out_shape=[full, full],
        compiler_params=params(),
        cost_estimate=pl.CostEstimate(flops=30 * rows * cols, bytes_accessed=20 * rows * cols, transcendentals=0),
    )(here_a, here_b, there_a, there_b, master, momentum)


def cost_of(blocks, rows):
    depth, cols = blocks[0].shape
    count = len(blocks)
    return pl.CostEstimate(
        flops=2 * rows * cols * depth * count, bytes_accessed=2 * count * depth * (cols + rows), transcendentals=0
    )


def own_kernel(first, count, whole, *refs):
    blocks, out = refs[:count], refs[-1]
    total = refs[count][...] if len(refs) > count + 1 else jnp.zeros(out.shape, jnp.float32)
    for k, block in enumerate(blocks):
        total += jnp.dot(whole[first + k], block[...], preferred_element_type=jnp.float32)
    out[...] = total


def dot_own(first, whole, blocks, *total):
    return pl.pallas_call(
        functools.partial(own_kernel, first, len(blocks)),
        in_specs=[VMEM] * (1 + len(blocks) + len(total)),
        out_specs=VMEM,
        out_shape=jax.ShapeDtypeStruct((whole.shape[1], blocks[0].shape[1]), jnp.float32),
        compiler_params=params(),
        cost_estimate=cost_of(blocks, whole.shape[1]),
    )(whole, *blocks, *total)


def early_kernel(start, count, own, other, *refs):
    blocks, total = refs[:count], refs[-1]
    total[...] = refs[count][...] if len(refs) > count + 1 else jnp.zeros(total.shape, jnp.float32)
    for k, block in enumerate(blocks):
        left = jnp.concatenate([own[start + k], other[start + k]], axis=0)
        total[...] += jnp.dot(left, block[...], preferred_element_type=jnp.float32)


def dot_early(start, own, other, blocks, *total):
    shape = (2 * own.shape[1], blocks[0].shape[1])
    return pl.pallas_call(
        functools.partial(early_kernel, start, len(blocks)),
        in_specs=[VMEM] * (2 + len(blocks) + len(total)),
        out_specs=VMEM,
        out_shape=jax.ShapeDtypeStruct(shape, jnp.float32),
        compiler_params=params(),
        cost_estimate=cost_of(blocks, shape[0]),
    )(own, other, *blocks, *total)


def late_kernel(start, own, other, early, *refs):
    *blocks, mine_part, sent_part = refs
    rows = own.shape[1]
    total = early[...]
    for k, block in enumerate(blocks):
        left = jnp.concatenate([own[start + k], other[start + k]], axis=0)
        total += jnp.dot(left, block[...], preferred_element_type=jnp.float32)
    mine_part[...] = total[:rows]
    sent_part[...] = total[rows:].astype(sent_part.dtype)


def dot_late(start, own, other, early, blocks):
    shape = (own.shape[1], blocks[0].shape[1])
    return pl.pallas_call(
        functools.partial(late_kernel, start),
        in_specs=[VMEM] * (3 + len(blocks)),
        out_specs=[VMEM] * 2,
        out_shape=[jax.ShapeDtypeStruct(shape, jnp.float32), jax.ShapeDtypeStruct(shape, jnp.bfloat16)],
        compiler_params=params(),
        cost_estimate=cost_of(blocks, 2 * shape[0]),
    )(own, other, early, *blocks)


def close_kernel(own_part, mine_part, other_part, inverse, keys):
    scale = jnp.broadcast_to(inverse[...], (inverse.shape[0], BLOCK))
    for col in range(0, keys.shape[1], BLOCK):
        at = slice(col, col + BLOCK)
        total = own_part[:, at] + mine_part[:, at] + other_part[:, at].astype(jnp.float32)
        keys[:, at] = (total * scale).astype(keys.dtype)


def close(own_part, mine_part, other_part, inverse):
    return pl.pallas_call(
        close_kernel,
        in_specs=[VMEM] * 4,
        out_specs=VMEM,
        out_shape=jax.ShapeDtypeStruct(mine_part.shape, jnp.bfloat16),
        compiler_params=params(),
    )(own_part, mine_part, other_part, inverse)


def by_permutes(tokens, norm_gain, master, momentum, pseudo_grad):
    chips = lax.axis_size("fsdp") // CORES
    ring = functools.partial(lax.ppermute, axis_name="fsdp", perm=ring_pairs(chips))
    swap = functools.partial(lax.ppermute, axis_name="fsdp", perm=swap_pairs(chips))
    cross = functools.partial(lax.ppermute, axis_name="island", perm=[(0, 1), (1, 0)])
    tie = lax.optimization_barrier

    gain = norm_gain.reshape(-1, BLOCK)
    half = master.shape[0] // 2
    sent_parts = cast_half(pseudo_grad[0], others, half // 2, half // 2)
    here_parts = [cross(part) for part in sent_parts]
    (grad_own,) = cast_half(pseudo_grad[0], mine, half)
    own, sent, more, whole, inverse = split_tokens(tokens, grad_own, chips)
    ready = get_ready(grad_own, master, momentum, gain)
    here_parts[0], own, *ready = tie((here_parts[0], own, *ready))
    other, more = cross(sent), cross(more)

    (head,) = half_weight(grad_own, here_parts[0], ready)
    tail, weight = half_weight(grad_own, here_parts[1], ready, head)
    swapped = swap(head)
    for _ in range(COPIES):
        swapped = join(swapped)
    b = near = join(swapped, swap(tail))
    blocks = []
    for step in range(1, chips // 2):
        if step == 1:
            arrived = ring(head)
            for _ in range(COPIES):
                arrived = join(arrived)
            a = join(arrived, ring(tail))
        else:
            a = ring(a)
        b = ring(b)
        blocks += [a, b, swap(a), swap(b)]
    a = ring(a)
    ahead = len(blocks) - 2 * CORES
    total = dot_early(0, own, other, blocks[:ahead])
    far, total = tie((a, total))
    late = [a, swap(far)]

    grad_sent, grad_here = join(*sent_parts), join(*here_parts)
    grad_there = unpack(len(slots(chips)[0]), other, more, grad_own.shape)
    weight_over = sync_weight(others, grad_sent, grad_there, master, momentum, gain)
    own_part = dot_own(0, whole, [weight, weight_over, near, swap(weight_over)])
    master_new, momentum_new = sync_outer(grad_own, grad_here, grad_sent, grad_there, master, momentum)
    total = dot_early(ahead, own, other, blocks[ahead:], total)
    mine_part, sent_part = dot_late(len(blocks), own, other, total, late)
    keys = close(own_part, mine_part, cross(sent_part), inverse)
    return (keys, master_new, momentum_new)


def by_gathers(tokens, norm_gain, master, momentum, pseudo_grad):
    islands = lax.axis_size("island")
    island_grad = pseudo_grad[0]
    row_total, col_total = island_grad.shape
    every_island = lax.all_gather(
        pseudo_grad.astype(jnp.bfloat16), "island", axis=0, tiled=True
    ).astype(pseudo_grad.dtype)
    grouped_all = every_island.reshape(islands, row_total, col_total // BLOCK, BLOCK)
    peaks_all = jnp.max(jnp.abs(grouped_all), axis=3)
    shared = jnp.sum(peaks_all, axis=0) / islands + 1e-06
    quantized_all = jnp.clip(grouped_all / shared[None, :, :, None], -1.0, 1.0).astype(jnp.bfloat16)
    summed = jnp.sum(quantized_all.astype(jnp.float32), axis=0)
    outer_grad = (shared[:, :, None] * summed / islands).reshape(row_total, col_total)
    momentum_new = outer_mu * momentum + outer_grad
    master_new = master - outer_rate * (outer_grad + outer_mu * momentum_new)
    weight = master_new.astype(jnp.bfloat16)
    features = tokens.astype(jnp.float32)
    inverse = lax.rsqrt(jnp.mean(features * features, axis=1, keepdims=True) + 1e-05)
    normed = (features * inverse * norm_gain[None, :]).astype(jnp.bfloat16)
    scale = 1.0 / jnp.sqrt(jnp.float32(normed.shape[1]))
    gathered = lax.all_gather(weight, "fsdp", axis=0, tiled=True)
    product = jnp.dot(normed, gathered, preferred_element_type=jnp.float32)
    keys = (product * scale).astype(jnp.bfloat16)
    return (keys, master_new, momentum_new)


def on_device(tokens, norm_gain, master, momentum, pseudo_grad):
    shards = lax.axis_size("fsdp")
    rows = master.shape[0]
    ringed = shards % (2 * CORES) == 0 and 4 * CORES <= shards <= RING_LIMIT * CORES
    tiled = tokens.shape[0] == BLOCK and rows % (2 * BLOCK) == 0 and 2 * master.shape[1] % rows == 0
    if lax.axis_size("island") == 2 and ringed and tiled:
        return by_permutes(tokens, norm_gain, master, momentum, pseudo_grad)
    return by_gathers(tokens, norm_gain, master, momentum, pseudo_grad)


def solution(mesh):
    placed = (
        P(("island", "fsdp"), None),
        P(),
        P("fsdp", None),
        P("fsdp", None),
        P("island", "fsdp", None),
    )
    return jax.shard_map(
        on_device,
        mesh=mesh,
        in_specs=placed,
        out_specs=(P(("island", "fsdp"), None), P("fsdp", None), P("fsdp", None)),
        check_vma=False,
    )
```

```python
import functools

import jax
import jax.numpy as jnp
from jax import lax
from jax.experimental import pallas as pl
from jax.experimental.pallas import tpu as pltpu
from jax.sharding import PartitionSpec as P

BLOCK = 128
CORES = 2
RING_LIMIT = 16
PACKED = 2
COPIES = 2

outer_rate = 0.7
outer_mu = 0.9
VMEM = pl.BlockSpec(memory_space=pltpu.VMEM)
VMEM_LIMIT = 40 * 1024 * 1024


def params():
    return pltpu.CompilerParams(vmem_limit_bytes=VMEM_LIMIT)


def chip_at(place, chips):
    up = 2 * place
    down = 2 * (chips - 1 - place) + 1
    if isinstance(place, int):
        return up if place < chips // 2 else down
    return jnp.where(place < chips // 2, up, down)


def place_of(chip, chips):
    if isinstance(chip, int):
        return chip // 2 if chip % 2 == 0 else chips - 1 - chip // 2
    return jnp.where(chip % 2 == 0, chip // 2, chips - 1 - chip // 2)


def ring_pairs(chips):
    pairs = []
    for chip in range(chips):
        for core in range(CORES):
            step = 1 if core == 0 else -1
            target = chip_at((place_of(chip, chips) + step) % chips, chips)
            pairs.append((chip * CORES + core, target * CORES + core))
    return pairs


def swap_pairs(chips):
    return [(f, f ^ 1) for f in range(CORES * chips)]


def slots(chips):
    shared = []
    for step in range(1, chips // 2):
        shared += [(step, 0), (step, 1), (-step, 1), (-step, 0)]
    return shared + [(chips // 2, 0), (chips // 2, 1)], [(0, 0), (0, 1)]


def shard_of(slot, chips):
    back, other = slot
    me = lax.axis_index("fsdp")
    core = me % CORES
    direction = jnp.where(core == 0, -1, 1)
    place = (place_of(me // CORES, chips) + direction * back + chips) % chips
    return chip_at(place, chips) * CORES + (1 - core if other else core)


def cast_kernel(grad, *outs):
    start = 0
    for out in outs:
        out[...] = grad[start : start + out.shape[0]].astype(out.dtype)
        start += out.shape[0]


def cast_half(grad, which, *heights):
    rows, cols = grad.shape
    half = rows // 2
    return pl.pallas_call(
        cast_kernel,
        grid=(1,),
        in_specs=[pl.BlockSpec((half, cols), lambda g: (which(), 0))],
        out_specs=[pl.BlockSpec((height, cols), lambda g: (0, 0)) for height in heights],
        out_shape=[jax.ShapeDtypeStruct((height, cols), jnp.bfloat16) for height in heights],
        compiler_params=params(),
        cost_estimate=pl.CostEstimate(flops=half * cols, bytes_accessed=6 * half * cols, transcendentals=0),
    )(grad)


def join_kernel(*refs):
    *parts, out = refs
    start = 0
    for part in parts:
        out[start : start + part.shape[0]] = part[...]
        start += part.shape[0]


def join(*parts):
    rows, cols = sum(part.shape[0] for part in parts), parts[0].shape[1]
    return pl.pallas_call(
        join_kernel,
        in_specs=[VMEM] * len(parts),
        out_specs=VMEM,
        out_shape=jax.ShapeDtypeStruct((rows, cols), parts[0].dtype),
        compiler_params=params(),
        cost_estimate=pl.CostEstimate(flops=0, bytes_accessed=4 * rows * cols, transcendentals=0),
    )(*parts)


def mine():
    return lax.axis_index("island")


def others():
    return 1 - lax.axis_index("island")


def tiles(shape, tall, wide):
    rows, cols = shape
    return [(slice(r, r + tall), slice(c, c + wide)) for r in range(0, rows, tall) for c in range(0, cols, wide)]


def token_kernel(chips, half, tokens, grad, own, sent, more, whole, inverse):
    rows, width = tokens.shape
    shared, kept = slots(chips)

    def columns(slot, which):
        start = shard_of(slot, chips) * 2 * half + which * half
        return tokens[:, pl.ds(pl.multiple_of(start, half), half)]

    for k, slot in enumerate(shared):
        own[k] = columns(slot, mine())
        sent[k] = columns(slot, others())
    for k, at in enumerate(tiles(grad.shape, rows, half)):
        if k < PACKED:
            sent[len(shared) + k] = grad[at]
        else:
            more[k - PACKED] = grad[at]
    for k, slot in enumerate(kept):
        whole[2 * k] = columns(slot, mine())
        whole[2 * k + 1] = columns(slot, others())
    total = jnp.zeros((rows, BLOCK), jnp.float32)
    for k in range(width // BLOCK):
        part = tokens[:, k * BLOCK : (k + 1) * BLOCK].astype(jnp.float32)
        total += part * part
    mean = jnp.sum(total, axis=1, keepdims=True) / width
    inverse[...] = lax.rsqrt(mean + 1e-05) / jnp.sqrt(jnp.float32(width))


def split_tokens(tokens, grad, chips):
    rows, width = tokens.shape
    half = width // (chips * CORES * 2)
    shared, kept = slots(chips)
    count = len(tiles(grad.shape, rows, half))
    counts = len(shared), len(shared) + PACKED, count - PACKED, 2 * len(kept)
    return pl.pallas_call(
        functools.partial(token_kernel, chips, half),
        in_specs=[VMEM] * 2,
        out_specs=[VMEM] * 5,
        out_shape=[jax.ShapeDtypeStruct((count, rows, half), tokens.dtype) for count in counts]
        + [jax.ShapeDtypeStruct((rows, 1), jnp.float32)],
        compiler_params=params(),
        cost_estimate=pl.CostEstimate(flops=2 * rows * width, bytes_accessed=4 * rows * width, transcendentals=0),
    )(tokens, grad)


def unpack_kernel(first, packed, more, grad):
    count = packed.shape[0] - first
    for k, at in enumerate(tiles(grad.shape, *packed.shape[1:])):
        grad[at] = packed[first + k] if k < count else more[k - count]


def unpack(first, packed, more, shape):
    return pl.pallas_call(
        functools.partial(unpack_kernel, first),
        in_specs=[VMEM] * 2,
        out_specs=VMEM,
        out_shape=jax.ShapeDtypeStruct(shape, packed.dtype),
        compiler_params=params(),
        cost_estimate=pl.CostEstimate(flops=0, bytes_accessed=4 * shape[0] * shape[1], transcendentals=0),
    )(packed, more)


def synced(a, b):
    a, b = a.astype(jnp.float32), b.astype(jnp.float32)
    peak_a = jnp.max(jnp.abs(a), axis=1, keepdims=True)
    peak_b = jnp.max(jnp.abs(b), axis=1, keepdims=True)
    shared = (peak_a + peak_b) / 2 + 1e-06
    over = 1.0 / shared
    low_a = jnp.clip(a * over, -1.0, 1.0).astype(jnp.bfloat16).astype(jnp.float32)
    low_b = jnp.clip(b * over, -1.0, 1.0).astype(jnp.bfloat16).astype(jnp.float32)
    return shared * (low_a + low_b) / 2


def gains_of(gain, row):
    return jnp.transpose(jnp.broadcast_to(gain[pl.ds(row // BLOCK, 1), :], (BLOCK, BLOCK)))


def ready_kernel(own, master, momentum, gain, peaks, base, steep):
    half, cols = own.shape
    first = lax.axis_index("fsdp") * (2 * half)
    slope = -outer_rate * (1 + outer_mu)
    for start in range(0, half, BLOCK):
        rows = slice(start, start + BLOCK)
        there = mine() * half + start
        held = pl.ds(pl.multiple_of(there, BLOCK), BLOCK)
        gains = gains_of(gain, first + there)
        steep[rows, :] = gains * slope / 2
        for k, col in enumerate(range(0, cols, BLOCK)):
            at = slice(col, col + BLOCK)
            a = jnp.abs(own[rows, at].astype(jnp.float32))
            peaks[k, rows, :] = jnp.broadcast_to(jnp.max(a, axis=1, keepdims=True) / 2 + 1e-06, a.shape)
            base[rows, at] = gains * (master[held, at] - outer_rate * outer_mu * (outer_mu * momentum[held, at]))


def get_ready(own, master, momentum, gain):
    half, cols = own.shape
    shapes = (cols // BLOCK, half, BLOCK), (half, cols), (half, BLOCK)
    return pl.pallas_call(
        ready_kernel,
        in_specs=[VMEM] * 4,
        out_specs=[VMEM] * 3,
        out_shape=[jax.ShapeDtypeStruct(shape, jnp.float32) for shape in shapes],
        compiler_params=params(),
        cost_estimate=pl.CostEstimate(flops=8 * half * cols, bytes_accessed=18 * half * cols, transcendentals=0),
    )(own, master, momentum, gain)


def first_part(offset, own, here, peaks, base, steep, weight):
    rows = slice(offset, offset + here.shape[0])
    for k, col in enumerate(range(0, own.shape[1], BLOCK)):
        at = slice(col, col + BLOCK)
        a = own[rows, at].astype(jnp.float32)
        b = here[:, at].astype(jnp.float32)
        shared = peaks[k, rows, :] + jnp.max(jnp.abs(b), axis=1, keepdims=True) / 2
        over = 1.0 / shared
        low_a = jnp.clip(a * over, -1.0, 1.0).astype(jnp.bfloat16).astype(jnp.float32)
        low_b = jnp.clip(b * over, -1.0, 1.0).astype(jnp.bfloat16).astype(jnp.float32)
        weight[:, at] = (base[rows, at] + steep[rows, :] * shared * (low_a + low_b)).astype(weight.dtype)


def first_kernel(own, here, peaks, base, steep, weight):
    first_part(0, own, here, peaks, base, steep, weight)


def second_kernel(own, here, peaks, base, steep, done, weight, whole):
    offset = done.shape[0]
    first_part(offset, own, here, peaks, base, steep, weight)
    whole[:offset] = done[...]
    whole[offset:] = weight[...]


def half_weight(own, here, ready, *done):
    rows, cols = here.shape
    shapes = [(rows, cols)] + [(part.shape[0] + rows, cols) for part in done]
    return pl.pallas_call(
        second_kernel if done else first_kernel,
        in_specs=[VMEM] * (5 + len(done)),
        out_specs=[VMEM] * len(shapes),
        out_shape=[jax.ShapeDtypeStruct(shape, jnp.bfloat16) for shape in shapes],
        compiler_params=params(),
        cost_estimate=pl.CostEstimate(flops=20 * rows * cols, bytes_accessed=14 * rows * cols, transcendentals=0),
    )(own, here, *ready, *done)


def weight_kernel(which, first, second, master, momentum, gain, weight):
    half, cols = first.shape
    base = lax.axis_index("fsdp") * (2 * half)
    for start in range(0, half, BLOCK):
        rows = slice(start, start + BLOCK)
        there = which() * half + start
        held = pl.ds(pl.multiple_of(there, BLOCK), BLOCK)
        gains = gains_of(gain, base + there)
        for col in range(0, cols, BLOCK):
            at = slice(col, col + BLOCK)
            outer_grad = synced(first[rows, at], second[rows, at])
            still = master[held, at] - (outer_rate * outer_mu * outer_mu) * momentum[held, at]
            fresh = still - (outer_rate * (1 + outer_mu)) * outer_grad
            weight[rows, at] = (gains * fresh).astype(weight.dtype)


def sync_weight(which, first, second, master, momentum, gain):
    half, cols = first.shape
    return pl.pallas_call(
        functools.partial(weight_kernel, which),
        in_specs=[VMEM] * 5,
        out_specs=VMEM,
        out_shape=jax.ShapeDtypeStruct((half, cols), jnp.bfloat16),
        compiler_params=params(),
        cost_estimate=pl.CostEstimate(
            flops=30 * half * cols, bytes_accessed=14 * half * cols, transcendentals=0
        ),
    )(first, second, master, momentum, gain)


def outer_kernel(here_a, here_b, there_a, there_b, master, momentum, master_new, momentum_new):
    half, cols = here_a.shape
    for which, a, b in ((mine(), here_a, here_b), (others(), there_a, there_b)):
        for start in range(0, half, BLOCK):
            rows = slice(start, start + BLOCK)
            held = pl.ds(pl.multiple_of(which * half + start, BLOCK), BLOCK)
            for col in range(0, cols, BLOCK):
                at = slice(col, col + BLOCK)
                outer_grad = synced(a[rows, at], b[rows, at])
                moved = outer_mu * momentum[held, at] + outer_grad
                momentum_new[held, at] = moved
                master_new[held, at] = master[held, at] - outer_rate * (outer_grad + outer_mu * moved)


def sync_outer(here_a, here_b, there_a, there_b, master, momentum):
    rows, cols = master.shape
    full = jax.ShapeDtypeStruct(master.shape, jnp.float32)
    return pl.pallas_call(
        outer_kernel,
        in_specs=[VMEM] * 6,
        out_specs=[VMEM] * 2,
        out_shape=[full, full],
        compiler_params=params(),
        cost_estimate=pl.CostEstimate(flops=30 * rows * cols, bytes_accessed=20 * rows * cols, transcendentals=0),
    )(here_a, here_b, there_a, there_b, master, momentum)


def cost_of(blocks, rows):
    depth, cols = blocks[0].shape
    count = len(blocks)
    return pl.CostEstimate(
        flops=2 * rows * cols * depth * count, bytes_accessed=2 * count * depth * (cols + rows), transcendentals=0
    )


def own_kernel(first, count, whole, *refs):
    blocks, out = refs[:count], refs[-1]
    total = refs[count][...] if len(refs) > count + 1 else jnp.zeros(out.shape, jnp.float32)
    for k, block in enumerate(blocks):
        total += jnp.dot(whole[first + k], block[...], preferred_element_type=jnp.float32)
    out[...] = total


def dot_own(first, whole, blocks, *total):
    return pl.pallas_call(
        functools.partial(own_kernel, first, len(blocks)),
        in_specs=[VMEM] * (1 + len(blocks) + len(total)),
        out_specs=VMEM,
        out_shape=jax.ShapeDtypeStruct((whole.shape[1], blocks[0].shape[1]), jnp.float32),
        compiler_params=params(),
        cost_estimate=cost_of(blocks, whole.shape[1]),
    )(whole, *blocks, *total)


def early_kernel(start, count, own, other, *refs):
    blocks, total = refs[:count], refs[-1]
    total[...] = refs[count][...] if len(refs) > count + 1 else jnp.zeros(total.shape, jnp.float32)
    for k, block in enumerate(blocks):
        left = jnp.concatenate([own[start + k], other[start + k]], axis=0)
        total[...] += jnp.dot(left, block[...], preferred_element_type=jnp.float32)


def dot_early(start, own, other, blocks, *total):
    shape = (2 * own.shape[1], blocks[0].shape[1])
    return pl.pallas_call(
        functools.partial(early_kernel, start, len(blocks)),
        in_specs=[VMEM] * (2 + len(blocks) + len(total)),
        out_specs=VMEM,
        out_shape=jax.ShapeDtypeStruct(shape, jnp.float32),
        compiler_params=params(),
        cost_estimate=cost_of(blocks, shape[0]),
    )(own, other, *blocks, *total)


def late_kernel(start, own, other, early, *refs):
    *blocks, mine_part, sent_part = refs
    rows = own.shape[1]
    total = early[...]
    for k, block in enumerate(blocks):
        left = jnp.concatenate([own[start + k], other[start + k]], axis=0)
        total += jnp.dot(left, block[...], preferred_element_type=jnp.float32)
    mine_part[...] = total[:rows]
    sent_part[...] = total[rows:].astype(sent_part.dtype)


def dot_late(start, own, other, early, blocks):
    shape = (own.shape[1], blocks[0].shape[1])
    return pl.pallas_call(
        functools.partial(late_kernel, start),
        in_specs=[VMEM] * (3 + len(blocks)),
        out_specs=[VMEM] * 2,
        out_shape=[jax.ShapeDtypeStruct(shape, jnp.float32), jax.ShapeDtypeStruct(shape, jnp.bfloat16)],
        compiler_params=params(),
        cost_estimate=cost_of(blocks, 2 * shape[0]),
    )(own, other, early, *blocks)


def close_kernel(own_part, mine_part, other_part, inverse, keys):
    scale = jnp.broadcast_to(inverse[...], (inverse.shape[0], BLOCK))
    for col in range(0, keys.shape[1], BLOCK):
        at = slice(col, col + BLOCK)
        total = own_part[:, at] + mine_part[:, at] + other_part[:, at].astype(jnp.float32)
        keys[:, at] = (total * scale).astype(keys.dtype)


def close(own_part, mine_part, other_part, inverse):
    return pl.pallas_call(
        close_kernel,
        in_specs=[VMEM] * 4,
        out_specs=VMEM,
        out_shape=jax.ShapeDtypeStruct(mine_part.shape, jnp.bfloat16),
        compiler_params=params(),
    )(own_part, mine_part, other_part, inverse)


def by_permutes(tokens, norm_gain, master, momentum, pseudo_grad):
    chips = lax.axis_size("fsdp") // CORES
    ring = functools.partial(lax.ppermute, axis_name="fsdp", perm=ring_pairs(chips))
    swap = functools.partial(lax.ppermute, axis_name="fsdp", perm=swap_pairs(chips))
    cross = functools.partial(lax.ppermute, axis_name="island", perm=[(0, 1), (1, 0)])
    tie = lax.optimization_barrier

    gain = norm_gain.reshape(-1, BLOCK)
    half = master.shape[0] // 2
    sent_parts = cast_half(pseudo_grad[0], others, half // 2, half // 2)
    here_parts = [cross(part) for part in sent_parts]
    (grad_own,) = cast_half(pseudo_grad[0], mine, half)
    own, sent, more, whole, inverse = split_tokens(tokens, grad_own, chips)
    ready = get_ready(grad_own, master, momentum, gain)
    here_parts[0], own, *ready = tie((here_parts[0], own, *ready))
    other, more = cross(sent), cross(more)

    (head,) = half_weight(grad_own, here_parts[0], ready)
    tail, weight = half_weight(grad_own, here_parts[1], ready, head)
    swapped = swap(head)
    for _ in range(COPIES):
        swapped = join(swapped)
    b = near = join(swapped, swap(tail))
    blocks = []
    for step in range(1, chips // 2):
        if step == 1:
            arrived = ring(head)
            for _ in range(COPIES):
                arrived = join(arrived)
            a = join(arrived, ring(tail))
        else:
            a = ring(a)
        b = ring(b)
        blocks += [a, b, swap(a), swap(b)]
    a = ring(a)
    ahead = len(blocks) - 2 * CORES
    total = dot_early(0, own, other, blocks[:ahead])
    far, total = tie((a, total))
    late = [a, swap(far)]

    grad_sent, grad_here = join(*sent_parts), join(*here_parts)
    grad_there = unpack(len(slots(chips)[0]), other, more, grad_own.shape)
    weight_over = sync_weight(others, grad_sent, grad_there, master, momentum, gain)
    own_part = dot_own(0, whole, [weight, weight_over, near, swap(weight_over)])
    master_new, momentum_new = sync_outer(grad_own, grad_here, grad_sent, grad_there, master, momentum)
    total = dot_early(ahead, own, other, blocks[ahead:], total)
    mine_part, sent_part = dot_late(len(blocks), own, other, total, late)
    keys = close(own_part, mine_part, cross(sent_part), inverse)
    return (keys, master_new, momentum_new)


def by_gathers(tokens, norm_gain, master, momentum, pseudo_grad):
    islands = lax.axis_size("island")
    island_grad = pseudo_grad[0]
    row_total, col_total = island_grad.shape
    every_island = lax.all_gather(
        pseudo_grad.astype(jnp.bfloat16), "island", axis=0, tiled=True
    ).astype(pseudo_grad.dtype)
    grouped_all = every_island.reshape(islands, row_total, col_total // BLOCK, BLOCK)
    peaks_all = jnp.max(jnp.abs(grouped_all), axis=3)
    shared = jnp.sum(peaks_all, axis=0) / islands + 1e-06
    quantized_all = jnp.clip(grouped_all / shared[None, :, :, None], -1.0, 1.0).astype(jnp.bfloat16)
    summed = jnp.sum(quantized_all.astype(jnp.float32), axis=0)
    outer_grad = (shared[:, :, None] * summed / islands).reshape(row_total, col_total)
    momentum_new = outer_mu * momentum + outer_grad
    master_new = master - outer_rate * (outer_grad + outer_mu * momentum_new)
    weight = master_new.astype(jnp.bfloat16)
    features = tokens.astype(jnp.float32)
    inverse = lax.rsqrt(jnp.mean(features * features, axis=1, keepdims=True) + 1e-05)
    normed = (features * inverse * norm_gain[None, :]).astype(jnp.bfloat16)
    scale = 1.0 / jnp.sqrt(jnp.float32(normed.shape[1]))
    gathered = lax.all_gather(weight, "fsdp", axis=0, tiled=True)
    product = jnp.dot(normed, gathered, preferred_element_type=jnp.float32)
    keys = (product * scale).astype(jnp.bfloat16)
    return (keys, master_new, momentum_new)


def on_device(tokens, norm_gain, master, momentum, pseudo_grad):
    shards = lax.axis_size("fsdp")
    rows = master.shape[0]
    ringed = shards % (2 * CORES) == 0 and 4 * CORES <= shards <= RING_LIMIT * CORES
    tiled = tokens.shape[0] == BLOCK and rows % (2 * BLOCK) == 0 and 2 * master.shape[1] % rows == 0
    if lax.axis_size("island") == 2 and ringed and tiled:
        return by_permutes(tokens, norm_gain, master, momentum, pseudo_grad)
    return by_gathers(tokens, norm_gain, master, momentum, pseudo_grad)


def solution(mesh):
    placed = (
        P(("island", "fsdp"), None),
        P(),
        P("fsdp", None),
        P("fsdp", None),
        P("island", "fsdp", None),
    )
    return jax.shard_map(
        on_device,
        mesh=mesh,
        in_specs=placed,
        out_specs=(P(("island", "fsdp"), None), P("fsdp", None), P("fsdp", None)),
        check_vma=False,
    )
```

```python
import functools

import jax
import jax.numpy as jnp
from jax import lax
from jax.experimental import pallas as pl
from jax.experimental.pallas import tpu as pltpu
from jax.sharding import PartitionSpec as P

BLOCK = 128
CORES = 2
RING_LIMIT = 16
PACKED = 2
COPIES = 2

outer_rate = 0.7
outer_mu = 0.9
VMEM = pl.BlockSpec(memory_space=pltpu.VMEM)
VMEM_LIMIT = 40 * 1024 * 1024


def params():
    return pltpu.CompilerParams(vmem_limit_bytes=VMEM_LIMIT)


def chip_at(place, chips):
    up = 2 * place
    down = 2 * (chips - 1 - place) + 1
    if isinstance(place, int):
        return up if place < chips // 2 else down
    return jnp.where(place < chips // 2, up, down)


def place_of(chip, chips):
    if isinstance(chip, int):
        return chip // 2 if chip % 2 == 0 else chips - 1 - chip // 2
    return jnp.where(chip % 2 == 0, chip // 2, chips - 1 - chip // 2)


def ring_pairs(chips):
    pairs = []
    for chip in range(chips):
        for core in range(CORES):
            step = 1 if core == 0 else -1
            target = chip_at((place_of(chip, chips) + step) % chips, chips)
            pairs.append((chip * CORES + core, target * CORES + core))
    return pairs


def swap_pairs(chips):
    return [(f, f ^ 1) for f in range(CORES * chips)]


def slots(chips):
    shared = []
    for step in range(1, chips // 2):
        shared += [(step, 0), (step, 1), (-step, 1), (-step, 0)]
    return shared + [(chips // 2, 0), (chips // 2, 1)], [(0, 0), (0, 1)]


def shard_of(slot, chips):
    back, other = slot
    me = lax.axis_index("fsdp")
    core = me % CORES
    direction = jnp.where(core == 0, -1, 1)
    place = (place_of(me // CORES, chips) + direction * back + chips) % chips
    return chip_at(place, chips) * CORES + (1 - core if other else core)


def cast_kernel(grad, *outs):
    start = 0
    for out in outs:
        out[...] = grad[start : start + out.shape[0]].astype(out.dtype)
        start += out.shape[0]


def cast_half(grad, which, *heights):
    rows, cols = grad.shape
    half = rows // 2
    return pl.pallas_call(
        cast_kernel,
        grid=(1,),
        in_specs=[pl.BlockSpec((half, cols), lambda g: (which(), 0))],
        out_specs=[pl.BlockSpec((height, cols), lambda g: (0, 0)) for height in heights],
        out_shape=[jax.ShapeDtypeStruct((height, cols), jnp.bfloat16) for height in heights],
        compiler_params=params(),
        cost_estimate=pl.CostEstimate(flops=half * cols, bytes_accessed=6 * half * cols, transcendentals=0),
    )(grad)


def join_kernel(*refs):
    *parts, out = refs
    start = 0
    for part in parts:
        out[start : start + part.shape[0]] = part[...]
        start += part.shape[0]


def join(*parts):
    rows, cols = sum(part.shape[0] for part in parts), parts[0].shape[1]
    return pl.pallas_call(
        join_kernel,
        in_specs=[VMEM] * len(parts),
        out_specs=VMEM,
        out_shape=jax.ShapeDtypeStruct((rows, cols), parts[0].dtype),
        compiler_params=params(),
        cost_estimate=pl.CostEstimate(flops=0, bytes_accessed=4 * rows * cols, transcendentals=0),
    )(*parts)


def mine():
    return lax.axis_index("island")


def others():
    return 1 - lax.axis_index("island")


def tiles(shape, tall, wide):
    rows, cols = shape
    return [(slice(r, r + tall), slice(c, c + wide)) for r in range(0, rows, tall) for c in range(0, cols, wide)]


def token_kernel(chips, half, tokens, grad, own, sent, more, whole, inverse):
    rows, width = tokens.shape
    shared, kept = slots(chips)

    def columns(slot, which):
        start = shard_of(slot, chips) * 2 * half + which * half
        return tokens[:, pl.ds(pl.multiple_of(start, half), half)]

    for k, slot in enumerate(shared):
        own[k] = columns(slot, mine())
        sent[k] = columns(slot, others())
    for k, at in enumerate(tiles(grad.shape, rows, half)):
        if k < PACKED:
            sent[len(shared) + k] = grad[at]
        else:
            more[k - PACKED] = grad[at]
    for k, slot in enumerate(kept):
        whole[2 * k] = columns(slot, mine())
        whole[2 * k + 1] = columns(slot, others())
    total = jnp.zeros((rows, BLOCK), jnp.float32)
    for k in range(width // BLOCK):
        part = tokens[:, k * BLOCK : (k + 1) * BLOCK].astype(jnp.float32)
        total += part * part
    mean = jnp.sum(total, axis=1, keepdims=True) / width
    inverse[...] = lax.rsqrt(mean + 1e-05) / jnp.sqrt(jnp.float32(width))


def split_tokens(tokens, grad, chips):
    rows, width = tokens.shape
    half = width // (chips * CORES * 2)
    shared, kept = slots(chips)
    count = len(tiles(grad.shape, rows, half))
    counts = len(shared), len(shared) + PACKED, count - PACKED, 2 * len(kept)
    return pl.pallas_call(
        functools.partial(token_kernel, chips, half),
        in_specs=[VMEM] * 2,
        out_specs=[VMEM] * 5,
        out_shape=[jax.ShapeDtypeStruct((count, rows, half), tokens.dtype) for count in counts]
        + [jax.ShapeDtypeStruct((rows, 1), jnp.float32)],
        compiler_params=params(),
        cost_estimate=pl.CostEstimate(flops=2 * rows * width, bytes_accessed=4 * rows * width, transcendentals=0),
    )(tokens, grad)


def unpack_kernel(first, packed, more, grad):
    count = packed.shape[0] - first
    for k, at in enumerate(tiles(grad.shape, *packed.shape[1:])):
        grad[at] = packed[first + k] if k < count else more[k - count]


def unpack(first, packed, more, shape):
    return pl.pallas_call(
        functools.partial(unpack_kernel, first),
        in_specs=[VMEM] * 2,
        out_specs=VMEM,
        out_shape=jax.ShapeDtypeStruct(shape, packed.dtype),
        compiler_params=params(),
        cost_estimate=pl.CostEstimate(flops=0, bytes_accessed=4 * shape[0] * shape[1], transcendentals=0),
    )(packed, more)


def synced(a, b):
    a, b = a.astype(jnp.float32), b.astype(jnp.float32)
    peak_a = jnp.max(jnp.abs(a), axis=1, keepdims=True)
    peak_b = jnp.max(jnp.abs(b), axis=1, keepdims=True)
    shared = (peak_a + peak_b) / 2 + 1e-06
    over = 1.0 / shared
    low_a = jnp.clip(a * over, -1.0, 1.0).astype(jnp.bfloat16).astype(jnp.float32)
    low_b = jnp.clip(b * over, -1.0, 1.0).astype(jnp.bfloat16).astype(jnp.float32)
    return shared * (low_a + low_b) / 2


def gains_of(gain, row):
    return jnp.transpose(jnp.broadcast_to(gain[pl.ds(row // BLOCK, 1), :], (BLOCK, BLOCK)))


def ready_kernel(own, master, momentum, gain, peaks, base, steep):
    half, cols = own.shape
    first = lax.axis_index("fsdp") * (2 * half)
    slope = -outer_rate * (1 + outer_mu)
    for start in range(0, half, BLOCK):
        rows = slice(start, start + BLOCK)
        there = mine() * half + start
        held = pl.ds(pl.multiple_of(there, BLOCK), BLOCK)
        gains = gains_of(gain, first + there)
        steep[rows, :] = gains * slope / 2
        for k, col in enumerate(range(0, cols, BLOCK)):
            at = slice(col, col + BLOCK)
            a = jnp.abs(own[rows, at].astype(jnp.float32))
            peaks[k, rows, :] = jnp.broadcast_to(jnp.max(a, axis=1, keepdims=True) / 2 + 1e-06, a.shape)
            base[rows, at] = gains * (master[held, at] - outer_rate * outer_mu * (outer_mu * momentum[held, at]))


def get_ready(own, master, momentum, gain):
    half, cols = own.shape
    shapes = (cols // BLOCK, half, BLOCK), (half, cols), (half, BLOCK)
    return pl.pallas_call(
        ready_kernel,
        in_specs=[VMEM] * 4,
        out_specs=[VMEM] * 3,
        out_shape=[jax.ShapeDtypeStruct(shape, jnp.float32) for shape in shapes],
        compiler_params=params(),
        cost_estimate=pl.CostEstimate(flops=8 * half * cols, bytes_accessed=18 * half * cols, transcendentals=0),
    )(own, master, momentum, gain)


def first_part(offset, own, here, peaks, base, steep, weight):
    rows = slice(offset, offset + here.shape[0])
    for k, col in enumerate(range(0, own.shape[1], BLOCK)):
        at = slice(col, col + BLOCK)
        a = own[rows, at].astype(jnp.float32)
        b = here[:, at].astype(jnp.float32)
        shared = peaks[k, rows, :] + jnp.max(jnp.abs(b), axis=1, keepdims=True) / 2
        over = 1.0 / shared
        low_a = jnp.clip(a * over, -1.0, 1.0).astype(jnp.bfloat16).astype(jnp.float32)
        low_b = jnp.clip(b * over, -1.0, 1.0).astype(jnp.bfloat16).astype(jnp.float32)
        weight[:, at] = (base[rows, at] + steep[rows, :] * shared * (low_a + low_b)).astype(weight.dtype)


def first_kernel(own, here, peaks, base, steep, weight):
    first_part(0, own, here, peaks, base, steep, weight)


def second_kernel(own, here, peaks, base, steep, done, weight, whole):
    offset = done.shape[0]
    first_part(offset, own, here, peaks, base, steep, weight)
    whole[:offset] = done[...]
    whole[offset:] = weight[...]


def half_weight(own, here, ready, *done):
    rows, cols = here.shape
    shapes = [(rows, cols)] + [(part.shape[0] + rows, cols) for part in done]
    return pl.pallas_call(
        second_kernel if done else first_kernel,
        in_specs=[VMEM] * (5 + len(done)),
        out_specs=[VMEM] * len(shapes),
        out_shape=[jax.ShapeDtypeStruct(shape, jnp.bfloat16) for shape in shapes],
        compiler_params=params(),
        cost_estimate=pl.CostEstimate(flops=20 * rows * cols, bytes_accessed=14 * rows * cols, transcendentals=0),
    )(own, here, *ready, *done)


def weight_kernel(which, first, second, master, momentum, gain, weight):
    half, cols = first.shape
    base = lax.axis_index("fsdp") * (2 * half)
    for start in range(0, half, BLOCK):
        rows = slice(start, start + BLOCK)
        there = which() * half + start
        held = pl.ds(pl.multiple_of(there, BLOCK), BLOCK)
        gains = gains_of(gain, base + there)
        for col in range(0, cols, BLOCK):
            at = slice(col, col + BLOCK)
            outer_grad = synced(first[rows, at], second[rows, at])
            moved = outer_mu * momentum[held, at] + outer_grad
            fresh = master[held, at] - outer_rate * (outer_grad + outer_mu * moved)
            weight[rows, at] = (gains * fresh).astype(weight.dtype)


def sync_weight(which, first, second, master, momentum, gain):
    half, cols = first.shape
    return pl.pallas_call(
        functools.partial(weight_kernel, which),
        in_specs=[VMEM] * 5,
        out_specs=VMEM,
        out_shape=jax.ShapeDtypeStruct((half, cols), jnp.bfloat16),
        compiler_params=params(),
        cost_estimate=pl.CostEstimate(
            flops=30 * half * cols, bytes_accessed=14 * half * cols, transcendentals=0
        ),
    )(first, second, master, momentum, gain)


def outer_kernel(here_a, here_b, there_a, there_b, master, momentum, master_new, momentum_new):
    half, cols = here_a.shape
    for which, a, b in ((mine(), here_a, here_b), (others(), there_a, there_b)):
        for start in range(0, half, BLOCK):
            rows = slice(start, start + BLOCK)
            held = pl.ds(pl.multiple_of(which * half + start, BLOCK), BLOCK)
            for col in range(0, cols, BLOCK):
                at = slice(col, col + BLOCK)
                outer_grad = synced(a[rows, at], b[rows, at])
                moved = outer_mu * momentum[held, at] + outer_grad
                momentum_new[held, at] = moved
                master_new[held, at] = master[held, at] - outer_rate * (outer_grad + outer_mu * moved)


def sync_outer(here_a, here_b, there_a, there_b, master, momentum):
    rows, cols = master.shape
    full = jax.ShapeDtypeStruct(master.shape, jnp.float32)
    return pl.pallas_call(
        outer_kernel,
        in_specs=[VMEM] * 6,
        out_specs=[VMEM] * 2,
        out_shape=[full, full],
        compiler_params=params(),
        cost_estimate=pl.CostEstimate(flops=30 * rows * cols, bytes_accessed=20 * rows * cols, transcendentals=0),
    )(here_a, here_b, there_a, there_b, master, momentum)


def cost_of(blocks, rows):
    depth, cols = blocks[0].shape
    count = len(blocks)
    return pl.CostEstimate(
        flops=2 * rows * cols * depth * count, bytes_accessed=2 * count * depth * (cols + rows), transcendentals=0
    )


def own_kernel(first, count, whole, *refs):
    blocks, out = refs[:count], refs[-1]
    total = refs[count][...] if len(refs) > count + 1 else jnp.zeros(out.shape, jnp.float32)
    for k, block in enumerate(blocks):
        total += jnp.dot(whole[first + k], block[...], preferred_element_type=jnp.float32)
    out[...] = total


def dot_own(first, whole, blocks, *total):
    return pl.pallas_call(
        functools.partial(own_kernel, first, len(blocks)),
        in_specs=[VMEM] * (1 + len(blocks) + len(total)),
        out_specs=VMEM,
        out_shape=jax.ShapeDtypeStruct((whole.shape[1], blocks[0].shape[1]), jnp.float32),
        compiler_params=params(),
        cost_estimate=cost_of(blocks, whole.shape[1]),
    )(whole, *blocks, *total)


def early_kernel(start, count, own, other, *refs):
    blocks, out = refs[:count], refs[-1]
    total = refs[count][...] if len(refs) > count + 1 else jnp.zeros(out.shape, jnp.float32)
    for k, block in enumerate(blocks):
        left = jnp.concatenate([own[start + k], other[start + k]], axis=0)
        total += jnp.dot(left, block[...], preferred_element_type=jnp.float32)
    out[...] = total


def dot_early(start, own, other, blocks, *total):
    shape = (2 * own.shape[1], blocks[0].shape[1])
    return pl.pallas_call(
        functools.partial(early_kernel, start, len(blocks)),
        in_specs=[VMEM] * (2 + len(blocks) + len(total)),
        out_specs=VMEM,
        out_shape=jax.ShapeDtypeStruct(shape, jnp.float32),
        compiler_params=params(),
        cost_estimate=cost_of(blocks, shape[0]),
    )(own, other, *blocks, *total)


def late_kernel(start, own, other, early, *refs):
    *blocks, mine_part, sent_part = refs
    rows = own.shape[1]
    total = early[...]
    for k, block in enumerate(blocks):
        left = jnp.concatenate([own[start + k], other[start + k]], axis=0)
        total += jnp.dot(left, block[...], preferred_element_type=jnp.float32)
    mine_part[...] = total[:rows]
    sent_part[...] = total[rows:].astype(sent_part.dtype)


def dot_late(start, own, other, early, blocks):
    shape = (own.shape[1], blocks[0].shape[1])
    return pl.pallas_call(
        functools.partial(late_kernel, start),
        in_specs=[VMEM] * (3 + len(blocks)),
        out_specs=[VMEM] * 2,
        out_shape=[jax.ShapeDtypeStruct(shape, jnp.float32), jax.ShapeDtypeStruct(shape, jnp.bfloat16)],
        compiler_params=params(),
        cost_estimate=cost_of(blocks, 2 * shape[0]),
    )(own, other, early, *blocks)


def close_kernel(own_part, mine_part, other_part, inverse, keys):
    scale = jnp.broadcast_to(inverse[...], (inverse.shape[0], BLOCK))
    for col in range(0, keys.shape[1], BLOCK):
        at = slice(col, col + BLOCK)
        total = own_part[:, at] + mine_part[:, at] + other_part[:, at].astype(jnp.float32)
        keys[:, at] = (total * scale).astype(keys.dtype)


def close(own_part, mine_part, other_part, inverse):
    return pl.pallas_call(
        close_kernel,
        in_specs=[VMEM] * 4,
        out_specs=VMEM,
        out_shape=jax.ShapeDtypeStruct(mine_part.shape, jnp.bfloat16),
        compiler_params=params(),
    )(own_part, mine_part, other_part, inverse)


def by_permutes(tokens, norm_gain, master, momentum, pseudo_grad):
    chips = lax.axis_size("fsdp") // CORES
    ring = functools.partial(lax.ppermute, axis_name="fsdp", perm=ring_pairs(chips))
    swap = functools.partial(lax.ppermute, axis_name="fsdp", perm=swap_pairs(chips))
    cross = functools.partial(lax.ppermute, axis_name="island", perm=[(0, 1), (1, 0)])
    tie = lax.optimization_barrier

    gain = norm_gain.reshape(-1, BLOCK)
    half = master.shape[0] // 2
    sent_parts = cast_half(pseudo_grad[0], others, half // 2, half // 2)
    here_parts = [cross(part) for part in sent_parts]
    (grad_own,) = cast_half(pseudo_grad[0], mine, half)
    own, sent, more, whole, inverse = split_tokens(tokens, grad_own, chips)
    ready = get_ready(grad_own, master, momentum, gain)
    here_parts[0], own, *ready = tie((here_parts[0], own, *ready))
    other, more = cross(sent), cross(more)

    (head,) = half_weight(grad_own, here_parts[0], ready)
    tail, weight = half_weight(grad_own, here_parts[1], ready, head)
    swapped = swap(head)
    for _ in range(COPIES):
        swapped = join(swapped)
    b = near = join(swapped, swap(tail))
    blocks = []
    for step in range(1, chips // 2):
        if step == 1:
            arrived = ring(head)
            for _ in range(COPIES):
                arrived = join(arrived)
            a = join(arrived, ring(tail))
        else:
            a = ring(a)
        b = ring(b)
        blocks += [a, b, swap(a), swap(b)]
    a = ring(a)
    ahead = len(blocks) - 2 * CORES
    total = dot_early(0, own, other, blocks[:ahead])
    far, total = tie((a, total))
    late = [a, swap(far)]

    grad_sent, grad_here = join(*sent_parts), join(*here_parts)
    grad_there = unpack(len(slots(chips)[0]), other, more, grad_own.shape)
    weight_over = sync_weight(others, grad_sent, grad_there, master, momentum, gain)
    own_part = dot_own(0, whole, [weight, weight_over, near, swap(weight_over)])
    master_new, momentum_new = sync_outer(grad_own, grad_here, grad_sent, grad_there, master, momentum)
    total = dot_early(ahead, own, other, blocks[ahead:], total)
    mine_part, sent_part = dot_late(len(blocks), own, other, total, late)
    keys = close(own_part, mine_part, cross(sent_part), inverse)
    return (keys, master_new, momentum_new)


def by_gathers(tokens, norm_gain, master, momentum, pseudo_grad):
    islands = lax.axis_size("island")
    island_grad = pseudo_grad[0]
    row_total, col_total = island_grad.shape
    every_island = lax.all_gather(
        pseudo_grad.astype(jnp.bfloat16), "island", axis=0, tiled=True
    ).astype(pseudo_grad.dtype)
    grouped_all = every_island.reshape(islands, row_total, col_total // BLOCK, BLOCK)
    peaks_all = jnp.max(jnp.abs(grouped_all), axis=3)
    shared = jnp.sum(peaks_all, axis=0) / islands + 1e-06
    quantized_all = jnp.clip(grouped_all / shared[None, :, :, None], -1.0, 1.0).astype(jnp.bfloat16)
    summed = jnp.sum(quantized_all.astype(jnp.float32), axis=0)
    outer_grad = (shared[:, :, None] * summed / islands).reshape(row_total, col_total)
    momentum_new = outer_mu * momentum + outer_grad
    master_new = master - outer_rate * (outer_grad + outer_mu * momentum_new)
    weight = master_new.astype(jnp.bfloat16)
    features = tokens.astype(jnp.float32)
    inverse = lax.rsqrt(jnp.mean(features * features, axis=1, keepdims=True) + 1e-05)
    normed = (features * inverse * norm_gain[None, :]).astype(jnp.bfloat16)
    scale = 1.0 / jnp.sqrt(jnp.float32(normed.shape[1]))
    gathered = lax.all_gather(weight, "fsdp", axis=0, tiled=True)
    product = jnp.dot(normed, gathered, preferred_element_type=jnp.float32)
    keys = (product * scale).astype(jnp.bfloat16)
    return (keys, master_new, momentum_new)


def on_device(tokens, norm_gain, master, momentum, pseudo_grad):
    shards = lax.axis_size("fsdp")
    rows = master.shape[0]
    ringed = shards % (2 * CORES) == 0 and 4 * CORES <= shards <= RING_LIMIT * CORES
    tiled = tokens.shape[0] == BLOCK and rows % (2 * BLOCK) == 0 and 2 * master.shape[1] % rows == 0
    if lax.axis_size("island") == 2 and ringed and tiled:
        return by_permutes(tokens, norm_gain, master, momentum, pseudo_grad)
    return by_gathers(tokens, norm_gain, master, momentum, pseudo_grad)


def solution(mesh):
    placed = (
        P(("island", "fsdp"), None),
        P(),
        P("fsdp", None),
        P("fsdp", None),
        P("island", "fsdp", None),
    )
    return jax.shard_map(
        on_device,
        mesh=mesh,
        in_specs=placed,
        out_specs=(P(("island", "fsdp"), None), P("fsdp", None), P("fsdp", None)),
        check_vma=False,
    )
```
